32 devices in a mesh: grp: 16 (over z, y, x), tp: 2 (over core).
Axes of the slice: x: 2, y: 2, z: 4, core: 2. Of those that a mesh axis runs over, the one named last changes fastest.
Arguments:
- normed_token_input: bfloat16 [16384, 4096], P('grp', 'tp'), may hold values from -6 to 6
- queries: bfloat16 [16384, 4096], P('grp', 'tp'), may hold values from -6 to 6
- fresh_token_keys: bfloat16 [16384, 1024], P('grp', 'tp'), may hold values from -6 to 6
- fresh_token_values: bfloat16 [16384, 1024], P('grp', 'tp'), may hold values from -6 to 6
- token_request_index: int32 [16384], P('grp'), may hold values from 0 to 63, never falling along the last dimension, each value on 1 to 1024 neighbouring positions
- prefix_page_cache: bfloat16 [32, 2, 128, 1024], P('grp', None, None, 'tp'), may hold values from -6 to 6
- adapter_down_weight: bfloat16 [32, 16, 4096], P('grp', None, 'tp'), may hold values from -0.09375 to 0.09375
- adapter_up_weight: bfloat16 [32, 16, 4096], P('grp', None, 'tp'), may hold values from -1.5 to 1.5
- group_page_list: int32 [16, 4], replicated, may hold values from 0 to 31, as said below
- group_adapter_list: int32 [16, 4], replicated, may hold values from 0 to 31, as said below
- page_entry_index: int32 [64], replicated, may hold values from 0 to 3
- adapter_entry_index: int32 [64], replicated, may hold values from 0 to 3
Outputs:
- attended: bfloat16 [16384, 4096], P('grp', 'tp')
The draws below stay inside these ranges and needn't reach their ends.
Inputs may be any that keep to these rules, and one draw needn't show every extreme that they name: `group_page_list`: the 4 pages of a row lie with distinct owners: page // 2 differs within a row. `group_adapter_list`: the 4 adapters of a row lie with distinct owners: adapter // 2 differs within a row.
All inputs are finite; a program needn't handle non-finite values.
Results may differ from the reference program's by a relative error of at most 0.0065.
Values may be sent and summed in bfloat16 or wider, within the bound.
No kernel may reach another device: no remote copies, remote signals or barrier semaphores. Data moves between devices by JAX's collectives and lax.ppermute only.
A program may use at most 64 MiB of HBM per device.

```python
import math
import jax
import jax.numpy as jnp
import numpy as np
from jax import lax

MODEL_WIDTH = 4096
QUERY_HEADS = 32
KV_HEADS = 8
HEAD_WIDTH = 128
ADAPTER_RANK = 16
PAGE = 128
PG_USE = 4
ADAPTERS_LISTED = 4
SLOTS_DEV = 2
TOK_G = 1024
GROUPS = 16
TOKENS = 16384
POOL = 32
ADAPTER_TOTAL = 32
REQS = 64
QUERY_WIDTH = 4096
KVW = 1024


def build_table(key, salt, columns):
    folded = jax.random.fold_in(key, salt)
    first_key, second_key = jax.random.split(folded)
    starting = jax.random.randint(first_key, (GROUPS,), 0, GROUPS)
    starting = starting.at[0].set(GROUPS - 1)
    owners = (starting[:, None] + jnp.arange(columns, dtype=jnp.int32)[None, :]) % GROUPS
    within = jax.random.randint(second_key, (GROUPS, columns), 0, SLOTS_DEV)
    within = within.at[0, 0].set(SLOTS_DEV - 1).at[0, 1].set(0)
    return (owners * SLOTS_DEV + within).astype(jnp.int32)


def draw_group_page_list(key, part):
    return build_table(key, 11, PG_USE)


def draw_group_adapter_list(key, part):
    return build_table(key, 23, ADAPTERS_LISTED)


def draw_queries(key, part):
    base_key = jax.random.fold_in(key, 5)
    values = jnp.clip(jax.random.normal(base_key, (TOKENS, QUERY_HEADS * HEAD_WIDTH), jnp.float32), -6.0, 6.0)
    return values.astype(jnp.bfloat16)


def draw_prefix_page_cache(key, part):
    base_key = jax.random.fold_in(key, 9)
    array_shape = (POOL, 2, PAGE, KV_HEADS * HEAD_WIDTH)
    values = jnp.clip(jax.random.normal(base_key, array_shape, jnp.float32), -6.0, 6.0)
    return values.astype(jnp.bfloat16)


def touch_ends(entries, stream_key, smallest, top_value):
    index_at = [jax.random.randint(jax.random.fold_in(stream_key, axis), (), 0, length) for axis, length in enumerate(entries.shape)]
    widest = entries.shape.index(max(entries.shape))
    neighbour = index_at[:widest] + [(index_at[widest] + 1) % entries.shape[widest]] + index_at[widest + 1:]
    return entries.at[tuple(index_at)].set(smallest).at[tuple(neighbour)].set(top_value)


def block_scale(own_key, extent, cuts, least, largest):
    level = 1.0
    for dim, parts in cuts:
        draws = jax.random.uniform(jax.random.fold_in(jax.random.fold_in(own_key, 6), dim), (parts,), jnp.float32, least / len(cuts), largest / len(cuts))
        level = level * jnp.repeat(jnp.exp(draws), extent[dim] // parts).reshape((-1,) + (1,) * (len(extent) - 1 - dim))
    return level


def length_profile(number_of, total, limit, skew):
    portions = [(1 << 20) // math.isqrt(standing ** skew) + 1 for standing in range(2, number_of + 1)]
    spare, counts = total - limit - (number_of - 1), [1] * (number_of - 1)
    while spare > 0:
        free = [i for i in range(number_of - 1) if counts[i] < limit]
        whole, left = sum([portions[i] for i in free]), spare
        for i in free:
            more = min(limit - counts[i], max(1, left * portions[i] // whole), spare)
            counts[i] = counts[i] + more
            spare = spare - more
    return np.array([limit] + counts)


def uneven_parts(stream_key, count, total, limit, slope):
    if count == 2:
        one = jax.random.randint(stream_key, (), max(1, total - limit), min(limit, total - 1) + 1)
        return jnp.stack([one, total - one])
    lengths = jnp.asarray(length_profile(count, total, limit, slope), jnp.int32)
    couples = (count - 1) // 2
    source_of, taker = lengths[1:1 + 2 * couples:2], lengths[2:2 + 2 * couples:2]
    slack = jnp.minimum(source_of - 1, limit - taker)
    moved = jax.random.randint(jax.random.fold_in(stream_key, 1), (couples,), 0, 1 << 20) % (slack + 1)
    lengths = lengths.at[1:1 + 2 * couples:2].set(source_of - moved).at[2:2 + 2 * couples:2].set(taker + moved)
    return lengths[jax.random.permutation(jax.random.fold_in(stream_key, 2), count)]


def bell_draw(key, dims, deviation, limit, cuts=(), held_as=jnp.bfloat16):
    array = jax.random.normal(key, dims, jnp.float32) * deviation
    if len(cuts) > 0:
        array = block_scale(key, dims, cuts, -0.22, 0.18) * array
    return jnp.clip(array, min=-limit, max=limit).astype(held_as)


def setup_inputs(seed: int = 0) -> dict:
    splits = jax.random.split(jax.random.key(seed), 13)
    return {
        "normed_token_input": bell_draw(splits[0], (TOKENS, MODEL_WIDTH), 1.0, 6.0, ((0, 16), (1, 2))),
        "queries": draw_queries(jax.random.fold_in(splits[12], 71), 0),
        "fresh_token_keys": bell_draw(splits[2], (TOKENS, KVW), 1.0, 6.0, ((0, 16), (1, 2))),
        "fresh_token_values": bell_draw(splits[3], (TOKENS, KVW), 1.0, 6.0, ((0, 16), (1, 2))),
        "token_request_index": jnp.searchsorted(jnp.cumsum(uneven_parts(splits[4], REQS, TOKENS, TOK_G, 1)), jnp.arange(TOKENS), side="right").astype(jnp.int32),
        "prefix_page_cache": draw_prefix_page_cache(jax.random.fold_in(splits[12], 71), 0),
        "adapter_down_weight": bell_draw(splits[6], (ADAPTER_TOTAL, ADAPTER_RANK, MODEL_WIDTH), MODEL_WIDTH ** -0.5, 0.09375, ((0, 16), (2, 2))),
        "adapter_up_weight": bell_draw(splits[7], (ADAPTER_TOTAL, ADAPTER_RANK, QUERY_WIDTH), ADAPTER_RANK ** -0.5, 1.5, ((0, 16), (2, 2))),
        "group_page_list": draw_group_page_list(jax.random.fold_in(splits[12], 71), 0),
        "group_adapter_list": draw_group_adapter_list(jax.random.fold_in(splits[12], 71), 0),
        "page_entry_index": touch_ends(jax.random.randint(splits[10], (REQS,), 0, PG_USE), jax.random.fold_in(splits[10], 1), 0, PG_USE - 1).astype(jnp.int32),
        "adapter_entry_index": touch_ends(jax.random.randint(splits[11], (REQS,), 0, ADAPTERS_LISTED), jax.random.fold_in(splits[11], 1), 0, ADAPTERS_LISTED - 1).astype(jnp.int32),
    }


adapter_scale = 0.5


def group_attention(query_rows, keys_all, values_all, visible):
    tokens = query_rows.shape[0]
    per_kv = QUERY_HEADS // KV_HEADS
    stacked = query_rows.reshape(tokens, QUERY_HEADS, HEAD_WIDTH).transpose(1, 0, 2)

    def one_head(position):
        query_head = lax.dynamic_index_in_dim(stacked, position, 0, keepdims=False)
        key_head = lax.dynamic_index_in_dim(keys_all, position // per_kv, 0, keepdims=False)
        value_head = lax.dynamic_index_in_dim(values_all, position // per_kv, 0, keepdims=False)
        scores = jnp.einsum("qd,kd->qk", query_head, key_head, preferred_element_type=jnp.float32)
        scores = jnp.where(visible, scores * (HEAD_WIDTH ** -0.5), jnp.float32(-1e30))
        highest = jnp.max(scores, axis=1, keepdims=True)
        expo = jnp.where(visible, jnp.exp(scores - highest), jnp.float32(0.0))
        weights = (expo / jnp.sum(expo, axis=1, keepdims=True)).astype(jnp.bfloat16)
        return jnp.dot(weights, value_head, preferred_element_type=jnp.float32).astype(jnp.bfloat16)

    result = lax.map(one_head, jnp.arange(QUERY_HEADS, dtype=jnp.int32))
    return result.transpose(1, 0, 2).reshape(tokens, QUERY_HEADS * HEAD_WIDTH)


def reference(normed_token_input, queries, fresh_token_keys, fresh_token_values, token_request_index, prefix_page_cache, adapter_down_weight, adapter_up_weight, group_page_list, group_adapter_list, page_entry_index, adapter_entry_index):
    groups = GROUPS
    kvw = KV_HEADS * HEAD_WIDTH
    hidden_g = normed_token_input.reshape(groups, TOK_G, MODEL_WIDTH)
    query_g = queries.reshape(groups, TOK_G, QUERY_HEADS * HEAD_WIDTH)
    keys_g = fresh_token_keys.reshape(groups, TOK_G, kvw)
    values_g = fresh_token_values.reshape(groups, TOK_G, kvw)
    segs_g = token_request_index.reshape(groups, TOK_G)
    keys_prev = jnp.concatenate([jnp.zeros_like(keys_g[:1]), keys_g[:-1]], 0)
    values_prev = jnp.concatenate([jnp.zeros_like(values_g[:1]), values_g[:-1]], 0)
    segs_prev = jnp.concatenate([jnp.zeros_like(segs_g[:1]), segs_g[:-1] + 1], 0)

    def one_group(inputs):
        hidden, query_base, keys, values, segs, prev_keys, prev_values, prev_segs, page_row, adapter_entry_row = inputs
        pages = prefix_page_cache[page_row]
        down_factors = adapter_down_weight[adapter_entry_row].reshape(ADAPTERS_LISTED * ADAPTER_RANK, MODEL_WIDTH)
        up_factors = adapter_up_weight[adapter_entry_row].reshape(ADAPTERS_LISTED * ADAPTER_RANK, QUERY_HEADS * HEAD_WIDTH)
        page_of = page_entry_index[segs]
        adapter_of = adapter_entry_index[segs]
        adapter_mask = (adapter_of[:, None] == jnp.arange(ADAPTERS_LISTED, dtype=jnp.int32)[None, :]).astype(jnp.float32)
        expanded = jnp.repeat(adapter_mask, ADAPTER_RANK, axis=1)
        lowrank = (jnp.dot(hidden, down_factors.T, preferred_element_type=jnp.float32) * expanded).astype(jnp.bfloat16)
        query_update = jnp.dot(lowrank, up_factors, preferred_element_type=jnp.float32)
        query_adapted = (query_base.astype(jnp.float32) + adapter_scale * query_update).astype(jnp.bfloat16)
        page_keys = pages[:, 0].reshape(PG_USE * PAGE, kvw)
        page_values = pages[:, 1].reshape(PG_USE * PAGE, kvw)
        keys_all = jnp.concatenate([page_keys, prev_keys, keys], 0).reshape(-1, KV_HEADS, HEAD_WIDTH).transpose(1, 0, 2)
        values_all = jnp.concatenate([page_values, prev_values, values], 0).reshape(-1, KV_HEADS, HEAD_WIDTH).transpose(1, 0, 2)
        page_cols = jnp.arange(PG_USE * PAGE, dtype=jnp.int32) // PAGE
        see_page = page_of[:, None] == page_cols[None, :]
        see_prev = prev_segs[None, :] == segs[:, None] + 1
        order = jnp.arange(TOK_G, dtype=jnp.int32)
        see_own = (segs[None, :] == segs[:, None]) & (order[None, :] <= order[:, None])
        visible = jnp.concatenate([see_page, see_prev, see_own], 1)
        return group_attention(query_adapted, keys_all, values_all, visible)

    result = lax.map(one_group, (hidden_g, query_g, keys_g, values_g, segs_g, keys_prev, values_prev, segs_prev, group_page_list, group_adapter_list))
    return result.reshape(TOKENS, QUERY_HEADS * HEAD_WIDTH)
```

```python
import math

import jax
import jax.numpy as jnp
from jax import lax
from jax.experimental import pallas as pl
from jax.experimental.pallas import tpu as pltpu
from jax.sharding import PartitionSpec as P

QUERY_HEADS = 32
KV_HEADS = 8
HEAD_WIDTH = 128
PAGE = 128
PER_KV = QUERY_HEADS // KV_HEADS

adapter_scale = 0.5

SCORE_SCALE = HEAD_WIDTH ** (-0.5) * math.log2(math.e)
UNSEEN = -1e30

ONES_ROWS = 16
STATE_ROWS = HEAD_WIDTH + ONES_ROWS
SUM_ROW = HEAD_WIDTH
MAX_ROW = HEAD_WIDTH + 8

VMEM_LIMIT = 48 * 1024 * 1024


def columns_of(groups):
    columns = 1
    while columns * columns < groups and groups % (2 * columns) == 0:
        columns *= 2
    return columns


def gather_column(own, groups, columns):
    rows = groups // columns
    down = [(i, i + columns) for i in range(groups - columns)]
    up = [(i + columns, i) for i in range(groups - columns)]
    from_below, from_above = [], []
    lower = upper = own
    for _ in range(rows - 1):
        lower = lax.ppermute(lower, "grp", down)
        upper = lax.ppermute(upper, "grp", up)
        from_below.append(lower)
        from_above.append(upper)
    return from_below[::-1] + [own] + from_above


def pick_units(wanted, stacks, name):
    count = wanted.shape[0]
    unit = stacks[0].shape[1:]

    def body(wanted_ref, *refs):
        sources = refs[: len(stacks)]
        outputs = refs[len(stacks) : len(stacks) + count]
        sems = refs[-1]
        for m in range(count):
            for k, source in enumerate(sources):

                @pl.when(wanted_ref[m, 0] == k)
                def _():
                    pltpu.make_async_copy(
                        source.at[wanted_ref[m, 1]], outputs[m], sems.at[m]
                    ).start()

        for m in range(count):
            pltpu.make_async_copy(sources[0].at[0], outputs[m], sems.at[m]).wait()

    return pl.pallas_call(
        body,
        out_shape=[jax.ShapeDtypeStruct(unit, stacks[0].dtype)] * count,
        in_specs=[pl.BlockSpec(memory_space=pltpu.SMEM)]
        + [pl.BlockSpec(memory_space=pl.ANY)] * len(stacks),
        out_specs=[pl.BlockSpec(memory_space=pl.ANY)] * count,
        scratch_shapes=[pltpu.SemaphoreType.DMA((count,))],
        name=name,
    )(wanted, *stacks)


def deliver(own, listed, groups, columns, name):
    rows = groups // columns
    stored = own.shape[0]
    entries = listed.shape[1]
    me = lax.axis_index("grp")
    row, column = me // columns, me % columns
    stacks = gather_column(own, groups, columns)

    owner = listed // stored
    place = listed % stored
    owner_row, owner_column = owner // columns, owner % columns
    same = owner_column[:, :, None] == owner_column[:, None, :]
    earlier = jnp.arange(entries)[None, :] < jnp.arange(entries)[:, None]
    rank = jnp.sum((same & earlier[None]).astype(jnp.int32), axis=2)
    rounds = jnp.max(rank) + 1

    masks = jnp.arange(columns, dtype=jnp.int32)
    partner = row * columns + (column ^ masks)
    partner_pick = (partner[:, None] == jnp.arange(groups)[None, :]).astype(jnp.int32)

    def of_partner(table):
        return jnp.sum(partner_pick[:, :, None] * table[None], axis=1)

    his_column, his_rank = of_partner(owner_column), of_partner(rank)
    his_stack = of_partner(owner_row) - row + rows - 1
    his_place = of_partner(place)

    def exchange(turn):
        here = ((his_column == column) & (his_rank == turn)).astype(jnp.int32)
        some = jnp.sum(here, axis=1)
        stack = jnp.sum(here * his_stack, axis=1) + (1 - some) * (rows - 1)
        wanted = jnp.stack([stack, jnp.sum(here * his_place, axis=1)], axis=1)
        units = pick_units(wanted, stacks, name)
        return [units[0]] + [
            lax.ppermute(units[m], "grp", [(i, i ^ m) for i in range(groups)])
            for m in range(1, columns)
        ]

    my_mask = his_column[0] ^ column
    my_rank = his_rank[0]
    first = my_rank == 0
    used = jnp.any(first[:, None] & (my_mask[:, None] == masks[None, :]), axis=0)
    free_order = jnp.cumsum(1 - used.astype(jnp.int32)) - 1
    later_order = jnp.cumsum(1 - first.astype(jnp.int32)) - 1
    fits = (~used)[None, :] & (free_order[None, :] == later_order[:, None])
    spare = jnp.sum(fits.astype(jnp.int32) * masks[None, :], axis=1)
    buffer_of = jnp.where(first, my_mask, spare)

    buffers = exchange(jnp.int32(0))

    def another(carry):
        turn, held = carry
        held = list(held)
        arrived = exchange(turn)
        for b in range(columns):
            for m in range(columns):
                lands = jnp.any((my_rank == turn) & (my_mask == m) & (buffer_of == b))
                held[b] = jnp.where(lands, arrived[m], held[b])
        return turn + 1, tuple(held)

    _, buffers = lax.while_loop(
        lambda carry: carry[0] < rounds, another, (jnp.int32(1), tuple(buffers))
    )
    return buffers, buffer_of


def low_rank_part(normed, factors, rank_width):
    tokens, width = normed.shape
    block = min(256, tokens)
    total = rank_width * len(factors)

    def body(x_ref, *refs):
        down = jnp.concatenate([f[:rank_width, :] for f in refs[:-1]], axis=0)
        refs[-1][...] = lax.dot_general(
            x_ref[...], down, (((1,), (1,)), ((), ())), preferred_element_type=jnp.float32
        )

    return pl.pallas_call(
        body,
        grid=(tokens // block,),
        out_shape=jax.ShapeDtypeStruct((tokens, total), jnp.float32),
        in_specs=[pl.BlockSpec((block, width), lambda i: (i, 0))]
        + [pl.BlockSpec(f.shape, lambda i: (0, 0)) for f in factors],
        out_specs=pl.BlockSpec((block, total), lambda i: (i, 0)),
        compiler_params=pltpu.CompilerParams(vmem_limit_bytes=VMEM_LIMIT),
        cost_estimate=pl.CostEstimate(
            flops=2 * tokens * width * total,
            bytes_accessed=2 * tokens * width,
            transcendentals=0,
        ),
        name="low_rank_part",
    )(normed, *factors)


def absorb(scores, values_t, acc_ref, max_ref, head):
    held = max_ref[head : head + 1, :]
    highest = jnp.maximum(held, jnp.max(scores, axis=0, keepdims=True))
    weights = jnp.exp2(scores - highest).astype(jnp.bfloat16)
    fade = jnp.exp2(held - highest)
    max_ref[head : head + 1, :] = highest
    acc_ref[head] = acc_ref[head] * fade + jnp.dot(
        values_t, weights, preferred_element_type=jnp.float32
    )


def scores_of(keys, query):
    return (
        lax.dot_general(
            keys, query, (((1,), (1,)), ((), ())), preferred_element_type=jnp.float32
        )
        * SCORE_SCALE
    )


def transposed(values):
    return values.astype(jnp.float32).T.astype(jnp.bfloat16)


def fresh_attention(
    queries, low_rank, factors, rank_width, keys_before, values_before, keys, values, begin
):
    tokens, width = queries.shape
    kv_local = keys.shape[1] // HEAD_WIDTH
    heads_local = width // HEAD_WIDTH
    span = PER_KV * HEAD_WIDTH
    block = min(256, tokens)
    tile = min(256, tokens)
    blocks = tokens // block
    first_tile = begin.reshape(blocks, block)[:, 0] // tile

    def body(first_ref, q_ref, lr_ref, kb_ref, vb_ref, k_ref, v_ref, begin_ref, *refs):
        factor_refs = refs[: len(factors)]
        state_ref, adapted_ref, keys_ref, values_ref, acc_ref, max_ref = refs[len(factors) :]
        step = pl.program_id(1)

        @pl.when(step == 0)
        def _():
            keys_ref[:tokens, :] = kb_ref[...]
            keys_ref[tokens:, :] = k_ref[...]
            values_ref[:HEAD_WIDTH, :tokens] = transposed(vb_ref[...])
            values_ref[:HEAD_WIDTH, tokens:] = transposed(v_ref[...])
            values_ref[HEAD_WIDTH:, :] = jnp.ones((ONES_ROWS, 2 * tokens), jnp.bfloat16)

        up = jnp.concatenate([f[rank_width:, :] for f in factor_refs], axis=0)
        update = jnp.dot(lr_ref[...], up, preferred_element_type=jnp.float32)
        adapted_ref[...] = (
            q_ref[...].astype(jnp.float32) + adapter_scale * update
        ).astype(jnp.bfloat16)

        acc_ref[...] = jnp.zeros_like(acc_ref)
        max_ref[...] = jnp.full_like(max_ref, UNSEEN)
        start = begin_ref[...]
        own = tokens + step * block + lax.broadcasted_iota(jnp.int32, (1, block), 1)

        def one_tile(number, _):
            at = pl.multiple_of(number * tile, tile)
            key_rows = keys_ref[pl.ds(at, tile), :]
            values_t = values_ref[:, pl.ds(at, tile)]
            position = at + lax.broadcasted_iota(jnp.int32, (tile, block), 0)
            seen = (position >= start) & (position <= own)
            for head in range(PER_KV):
                query = adapted_ref[:, head * HEAD_WIDTH : (head + 1) * HEAD_WIDTH]
                scores = jnp.where(seen, scores_of(key_rows, query), UNSEEN)
                absorb(scores, values_t, acc_ref, max_ref, head)
            return 0

        last = (tokens + (step + 1) * block + tile - 1) // tile
        lax.fori_loop(first_ref[step], last, one_tile, 0)
        for head in range(PER_KV):
            state_ref[head, :MAX_ROW, :] = acc_ref[head, :MAX_ROW, :]
            state_ref[head, MAX_ROW:, :] = jnp.broadcast_to(
                max_ref[head : head + 1, :], (STATE_ROWS - MAX_ROW, block)
            )

    by_head = lambda h, i, first: (0, h)
    by_block = lambda h, i, first: (i, h)
    whole = pl.BlockSpec((tokens, HEAD_WIDTH), by_head)
    return pl.pallas_call(
        body,
        grid_spec=pltpu.PrefetchScalarGridSpec(
            num_scalar_prefetch=1,
            grid=(kv_local, blocks),
            in_specs=[
                pl.BlockSpec((block, span), by_block),
                pl.BlockSpec((block, low_rank.shape[1]), lambda h, i, first: (i, 0)),
                whole,
                whole,
                whole,
                whole,
                pl.BlockSpec((1, block), lambda h, i, first: (0, i)),
            ]
            + [pl.BlockSpec((f.shape[0], span), by_head) for f in factors],
            out_specs=[
                pl.BlockSpec((PER_KV, STATE_ROWS, block), lambda h, i, first: (h, 0, i)),
                pl.BlockSpec((block, span), by_block),
            ],
            scratch_shapes=[
                pltpu.VMEM((2 * tokens, HEAD_WIDTH), jnp.bfloat16),
                pltpu.VMEM((STATE_ROWS, 2 * tokens), jnp.bfloat16),
                pltpu.VMEM((PER_KV, STATE_ROWS, block), jnp.float32),
                pltpu.VMEM((8, block), jnp.float32),
            ],
        ),
        out_shape=[
            jax.ShapeDtypeStruct((heads_local, STATE_ROWS, tokens), jnp.float32),
            jax.ShapeDtypeStruct((tokens, width), jnp.bfloat16),
        ],
        compiler_params=pltpu.CompilerParams(vmem_limit_bytes=VMEM_LIMIT),
        cost_estimate=pl.CostEstimate(
            flops=4 * tokens * tokens * width // 2,
            bytes_accessed=20 * 1024 * 1024,
            transcendentals=heads_local * tokens * tokens // 2,
        ),
        name="fresh_attention",
    )(
        first_tile,
        queries,
        low_rank,
        keys_before,
        values_before,
        keys,
        values,
        begin.reshape(1, tokens),
        *factors,
    )


def page_attention(state, adapted, buffers, page_buffer):
    tokens, width = adapted.shape
    span = PER_KV * HEAD_WIDTH
    kv_local = width // span
    block = min(256, tokens)
    blocks = tokens // block
    count = len(buffers)
    uses = jnp.any(
        page_buffer.reshape(blocks, block, 1) == jnp.arange(count)[None, None, :], axis=1
    ).astype(jnp.int32)

    def body(uses_ref, state_ref, q_ref, which_ref, *refs):
        page_refs = refs[:count]
        out_ref, values_ref, acc_ref, max_ref = refs[count:]
        step = pl.program_id(1)

        @pl.when(step == 0)
        def _():
            for b in range(count):
                values_ref[b, :HEAD_WIDTH, :] = transposed(page_refs[b][PAGE:, :])
                values_ref[b, HEAD_WIDTH:, :] = jnp.ones((ONES_ROWS, PAGE), jnp.bfloat16)

        for head in range(PER_KV):
            acc_ref[head] = state_ref[head]
            max_ref[head : head + 1, :] = state_ref[head, MAX_ROW : MAX_ROW + 1, :]
        which = which_ref[...]
        for b in range(count):

            @pl.when(uses_ref[step, b] != 0)
            def _():
                seen = which == b
                for head in range(PER_KV):
                    query = q_ref[:, head * HEAD_WIDTH : (head + 1) * HEAD_WIDTH]
                    scores = jnp.where(seen, scores_of(page_refs[b][:PAGE, :], query), UNSEEN)
                    absorb(scores, values_ref[b], acc_ref, max_ref, head)

        for head in range(PER_KV):
            result = acc_ref[head, :HEAD_WIDTH, :] / acc_ref[head, SUM_ROW : SUM_ROW + 1, :]
            out_ref[:, head * HEAD_WIDTH : (head + 1) * HEAD_WIDTH] = result.T.astype(
                jnp.bfloat16
            )

    return pl.pallas_call(
        body,
        grid_spec=pltpu.PrefetchScalarGridSpec(
            num_scalar_prefetch=1,
            grid=(kv_local, blocks),
            in_specs=[
                pl.BlockSpec((PER_KV, STATE_ROWS, block), lambda h, i, uses: (h, 0, i)),
                pl.BlockSpec((block, span), lambda h, i, uses: (i, h)),
                pl.BlockSpec((1, block), lambda h, i, uses: (0, i)),
            ]
            + [pl.BlockSpec((2 * PAGE, HEAD_WIDTH), lambda h, i, uses: (0, h))] * count,
            out_specs=pl.BlockSpec((block, span), lambda h, i, uses: (i, h)),
            scratch_shapes=[
                pltpu.VMEM((count, STATE_ROWS, PAGE), jnp.bfloat16),
                pltpu.VMEM((PER_KV, STATE_ROWS, block), jnp.float32),
                pltpu.VMEM((8, block), jnp.float32),
            ],
        ),
        out_shape=jax.ShapeDtypeStruct((tokens, width), jnp.bfloat16),
        compiler_params=pltpu.CompilerParams(vmem_limit_bytes=VMEM_LIMIT),
        cost_estimate=pl.CostEstimate(
            flops=8 * tokens * PAGE * width,
            bytes_accessed=18 * 1024 * 1024,
            transcendentals=2 * tokens * PAGE * width // HEAD_WIDTH,
        ),
        name="page_attention",
    )(uses, state, adapted, page_buffer.reshape(1, tokens), *buffers)


def local(
    normed_token_input,
    queries,
    fresh_token_keys,
    fresh_token_values,
    token_request_index,
    prefix_page_cache,
    adapter_down_weight,
    adapter_up_weight,
    group_page_list,
    group_adapter_list,
    page_entry_index,
    adapter_entry_index,
):
    groups = lax.axis_size("grp")
    columns = columns_of(groups)
    rank_width = adapter_down_weight.shape[1]
    stored_pages, _, page_tokens, key_width = prefix_page_cache.shape

    onward = [(i, i + 1) for i in range(groups - 1)]
    ids_before = lax.ppermute(token_request_index + 1, "grp", onward) - 1
    keys_before = lax.ppermute(fresh_token_keys, "grp", onward)
    values_before = lax.ppermute(fresh_token_values, "grp", onward)

    adapters = jnp.concatenate([adapter_down_weight, adapter_up_weight], axis=1)
    factors, adapter_buffer_of = deliver(
        adapters, group_adapter_list, groups, columns, "pick_adapters"
    )
    pages, page_buffer_of = deliver(
        prefix_page_cache.reshape(stored_pages, 2 * page_tokens, key_width),
        group_page_list,
        groups,
        columns,
        "pick_pages",
    )

    requests = jnp.arange(page_entry_index.shape[0], dtype=jnp.int32)
    member = token_request_index[:, None] == requests[None, :]

    def by_token(entry_index, buffer_of):
        entries = jnp.arange(buffer_of.shape[0], dtype=jnp.int32)
        chosen = jnp.sum(
            jnp.where(entry_index[:, None] == entries[None, :], buffer_of[None, :], 0), axis=1
        )
        return jnp.sum(jnp.where(member, chosen[None, :], 0), axis=1)

    adapter_buffer = by_token(adapter_entry_index, adapter_buffer_of)
    page_buffer = by_token(page_entry_index, page_buffer_of)

    both_ids = jnp.concatenate([ids_before, token_request_index])
    begin = jnp.sum(
        (both_ids[None, :] < token_request_index[:, None]).astype(jnp.int32), axis=1
    )

    partial = low_rank_part(normed_token_input, factors, rank_width)
    if lax.axis_size("tp") == 2:
        total = partial + lax.ppermute(partial, "tp", [(0, 1), (1, 0)])
    else:
        total = lax.psum(partial, "tp")
    lane_buffer = jnp.arange(total.shape[1], dtype=jnp.int32) // rank_width
    low_rank = jnp.where(
        adapter_buffer[:, None] == lane_buffer[None, :], total, 0.0
    ).astype(jnp.bfloat16)

    state, adapted = fresh_attention(
        queries,
        low_rank,
        factors,
        rank_width,
        keys_before,
        values_before,
        fresh_token_keys,
        fresh_token_values,
        begin,
    )
    return page_attention(state, adapted, pages, page_buffer)


def solution(mesh):
    placed = (
        P("grp", "tp"),
        P("grp", "tp"),
        P("grp", "tp"),
        P("grp", "tp"),
        P("grp"),
        P("grp", None, None, "tp"),
        P("grp", None, "tp"),
        P("grp", None, "tp"),
        P(),
        P(),
        P(),
        P(),
    )
    return jax.shard_map(
        local, mesh=mesh, in_specs=placed, out_specs=P("grp", "tp"), check_vma=False
    )
```

```python
import math

import jax
import jax.numpy as jnp
from jax import lax
from jax.experimental import pallas as pl
from jax.experimental.pallas import tpu as pltpu
from jax.sharding import PartitionSpec as P

QUERY_HEADS = 32
KV_HEADS = 8
HEAD_WIDTH = 128
PAGE = 128
PER_KV = QUERY_HEADS // KV_HEADS

adapter_scale = 0.5

SCORE_SCALE = HEAD_WIDTH ** (-0.5) * math.log2(math.e)
UNSEEN = -1e30

ONES_ROWS = 16
STATE_ROWS = HEAD_WIDTH + ONES_ROWS
SUM_ROW = HEAD_WIDTH
MAX_ROW = HEAD_WIDTH + 8

VMEM_LIMIT = 48 * 1024 * 1024


def columns_of(groups):
    columns = 1
    while columns * columns < groups and groups % (2 * columns) == 0:
        columns *= 2
    return columns


def held_until(arrays, others):
    together = lax.optimization_barrier(tuple(arrays) + tuple(others))
    return together[: len(arrays)]


def along_columns(steps, columns):
    return [(a * columns + c, b * columns + c) for a, b in steps for c in range(columns)]


OUTER = [(0, 1), (1, 0), (2, 3), (3, 2)]
MIDDLE = [(1, 2), (2, 1)]


class Column:

    def __init__(self, own, groups, columns):
        self.own, self.groups, self.columns = own, groups, columns
        self.rows = groups // columns

    def swap(self, shard, steps):
        return lax.ppermute(shard, "grp", along_columns(steps, self.columns))

    def first_step(self, others=()):
        if self.rows == 4:
            (own,) = held_until((self.own,), others)
            self.one, self.two = self.swap(own, OUTER), self.swap(own, MIDDLE)
            return (self.one, self.two)
        return ()

    def second_step(self):
        if self.rows == 4:
            self.three, self.four = self.swap(self.two, OUTER), self.swap(self.one, MIDDLE)
            return (self.three, self.four)
        return ()

    def third_step(self):
        if self.rows == 4:
            five = self.swap(self.four, OUTER)
            self.stacks = [self.own, self.one, self.two, self.three, self.four, five]
            self.table = ((0, 1, 3, 5), (1, 0, 2, 4), (4, 2, 0, 1), (5, 3, 1, 0))
            return
        rows, columns, groups = self.rows, self.columns, self.groups
        down = [(i, i + columns) for i in range(groups - columns)]
        up = [(i + columns, i) for i in range(groups - columns)]
        from_below, from_above = [], []
        lower = upper = self.own
        for _ in range(rows - 1):
            lower = lax.ppermute(lower, "grp", down)
            upper = lax.ppermute(upper, "grp", up)
            from_below.append(lower)
            from_above.append(upper)
        self.stacks = from_below[::-1] + [self.own] + from_above
        self.table = tuple(tuple(w - r + rows - 1 for w in range(rows)) for r in range(rows))


def plan(listed, turn, stored, columns, table, name):
    groups, entries = listed.shape
    rows = groups // columns

    def body(listed_ref, turn_ref, wanted_ref, lands_ref, buffer_ref, turns_ref):
        me = lax.axis_index("grp")
        row, column = lax.div(me, columns), lax.rem(me, columns)
        turn = turn_ref[0]
        one, zero = jnp.int32(1), jnp.int32(0)

        def unit(group, entry):
            number = listed_ref[group, entry]
            owner = lax.div(number, stored)
            return lax.div(owner, columns), lax.rem(owner, columns), lax.rem(number, stored)

        def rank_of(group):
            owner_columns = [unit(group, e)[1] for e in range(entries)]
            return [
                sum(
                    [jnp.where(owner_columns[f] == owner_columns[e], one, zero) for f in range(e)],
                    zero,
                )
                for e in range(entries)
            ]

        for m in range(columns):
            partner = row * columns + jnp.bitwise_xor(column, m)
            ranks = rank_of(partner)
            stack, place = zero, zero
            for e in range(entries):
                owner_row, owner_column, within = unit(partner, e)
                here = (owner_column == column) & (ranks[e] == turn)
                held = zero
                for r in range(rows):
                    for w in range(rows):
                        held = jnp.where((row == r) & (owner_row == w), table[r][w], held)
                stack = jnp.where(here, held, stack)
                place = jnp.where(here, within, place)
            wanted_ref[m, 0] = stack
            wanted_ref[m, 1] = place

        ranks = rank_of(me)
        masks = [jnp.bitwise_xor(unit(me, e)[1], column) for e in range(entries)]
        taken = [
            sum(
                [jnp.where((ranks[e] == 0) & (masks[e] == m), one, zero) for e in range(entries)],
                zero,
            )
            for m in range(columns)
        ]
        buffers = []
        later = zero
        for e in range(entries):
            free, spare = zero, zero
            for m in range(columns):
                spare = jnp.where((taken[m] == 0) & (free == later), m, spare)
                free = free + 1 - taken[m]
            buffers.append(jnp.where(ranks[e] == 0, masks[e], spare))
            later = later + jnp.where(ranks[e] == 0, zero, one)
            buffer_ref[e] = buffers[e]
        for b in range(columns):
            lands = jnp.int32(-1)
            for e in range(entries):
                lands = jnp.where((ranks[e] == turn) & (buffers[e] == b), masks[e], lands)
            lands_ref[b] = lands

        def deepest(group, most):
            for rank in rank_of(group):
                most = jnp.maximum(most, rank + 1)
            return most

        turns_ref[0] = lax.fori_loop(0, groups, deepest, one)

    smem = pl.BlockSpec(memory_space=pltpu.SMEM)
    return pl.pallas_call(
        body,
        out_shape=[
            jax.ShapeDtypeStruct((columns, 2), jnp.int32),
            jax.ShapeDtypeStruct((columns,), jnp.int32),
            jax.ShapeDtypeStruct((entries,), jnp.int32),
            jax.ShapeDtypeStruct((1,), jnp.int32),
        ],
        in_specs=[smem, smem],
        out_specs=[smem] * 4,
        name=name,
    )(listed, turn)


def pick_units(wanted, stacks, name):
    count = wanted.shape[0]
    unit = stacks[0].shape[1:]

    def body(wanted_ref, *refs):
        sources = refs[: len(stacks)]
        outputs = refs[len(stacks) : len(stacks) + count]
        sems = refs[-1]
        for m in range(count):
            for k, source in enumerate(sources):

                @pl.when(wanted_ref[m, 0] == k)
                def _():
                    pltpu.make_async_copy(
                        source.at[wanted_ref[m, 1]], outputs[m], sems.at[m]
                    ).start()

        for m in range(count):
            pltpu.make_async_copy(sources[0].at[0], outputs[m], sems.at[m]).wait()

    return pl.pallas_call(
        body,
        out_shape=[jax.ShapeDtypeStruct(unit, stacks[0].dtype)] * count,
        in_specs=[pl.BlockSpec(memory_space=pltpu.SMEM)]
        + [pl.BlockSpec(memory_space=pl.ANY)] * len(stacks),
        out_specs=[pl.BlockSpec(memory_space=pltpu.VMEM)] * count,
        scratch_shapes=[pltpu.SemaphoreType.DMA((count,))],
        compiler_params=pltpu.CompilerParams(vmem_limit_bytes=VMEM_LIMIT),
        name=name,
    )(wanted, *stacks)


def deliver(column, listed, name, others):
    groups, columns, table = column.groups, column.columns, column.table
    stored = column.own.shape[0]
    stacks = held_until(column.stacks, others)

    def exchange(turn):
        wanted, lands, buffer_of, turns = plan(
            listed, turn, stored, columns, table, "plan_" + name
        )
        units = pick_units(wanted, stacks, "pick_" + name)
        units = [units[0]] + [
            lax.ppermute(units[m], "grp", [(i, i ^ m) for i in range(groups)])
            for m in range(1, columns)
        ]
        return units, lands, buffer_of, turns

    buffers, _, buffer_of, turns = exchange(jnp.zeros((1,), jnp.int32))

    def another(carry):
        turn, held = carry
        held = list(held)
        units, lands, _, _ = exchange(turn)
        for b in range(columns):
            for m in range(columns):
                held[b] = jnp.where(lands[b] == m, units[m], held[b])
        return turn + 1, tuple(held)

    _, buffers = lax.while_loop(
        lambda carry: carry[0][0] < turns[0],
        another,
        (jnp.ones((1,), jnp.int32), tuple(buffers)),
    )
    return buffers, buffer_of


def low_rank_part(normed, factors, rank_width):
    tokens, width = normed.shape
    block = min(256, tokens)
    total = rank_width * len(factors)

    def body(x_ref, *refs):
        down = jnp.concatenate([f[:rank_width, :] for f in refs[:-1]], axis=0)
        refs[-1][...] = lax.dot_general(
            x_ref[...], down, (((1,), (1,)), ((), ())), preferred_element_type=jnp.float32
        )

    return pl.pallas_call(
        body,
        grid=(tokens // block,),
        out_shape=jax.ShapeDtypeStruct((tokens, total), jnp.float32),
        in_specs=[pl.BlockSpec((block, width), lambda i: (i, 0))]
        + [pl.BlockSpec(f.shape, lambda i: (0, 0)) for f in factors],
        out_specs=pl.BlockSpec((block, total), lambda i: (i, 0)),
        compiler_params=pltpu.CompilerParams(vmem_limit_bytes=VMEM_LIMIT),
        cost_estimate=pl.CostEstimate(flops=1, bytes_accessed=1, transcendentals=0),
        name="low_rank_part",
    )(normed, *factors)


def scores_of(keys, queries_t):
    return jnp.dot(keys, queries_t, preferred_element_type=jnp.float32) * SCORE_SCALE


def absorb(scores, values_t, acc_ref, max_ref, heads):
    held = [max_ref[h : h + 1, :] for h in heads]
    highest = [
        jnp.maximum(old, jnp.max(s, axis=0, keepdims=True)) for old, s in zip(held, scores)
    ]
    weights = [jnp.exp2(s - top).astype(jnp.bfloat16) for s, top in zip(scores, highest)]
    added = [jnp.dot(values_t, w, preferred_element_type=jnp.float32) for w in weights]
    sums = [
        acc_ref[h] * jnp.exp2(old - top) + more
        for h, old, top, more in zip(heads, held, highest, added)
    ]
    for h, top, total in zip(heads, highest, sums):
        acc_ref[h] = total
        max_ref[h : h + 1, :] = top


def transposed(values):
    return values.astype(jnp.float32).T.astype(jnp.bfloat16)


def head_rows(head):
    return slice(head * HEAD_WIDTH, (head + 1) * HEAD_WIDTH)


def visit_tiles(first, last, tile, scores_at, values_at, score_ref, acc_ref, max_ref, heads):
    def one_tile(number, _):
        scores = [score_ref[n] for n in range(len(heads))]
        ahead = scores_at(pl.multiple_of(jnp.minimum(number + 1, last - 1) * tile, tile))
        absorb(scores, values_at(pl.multiple_of(number * tile, tile)), acc_ref, max_ref, heads)
        for n in range(len(heads)):
            score_ref[n] = ahead[n]
        return 0

    for n, s in enumerate(scores_at(pl.multiple_of(first * tile, tile))):
        score_ref[n] = s
    lax.fori_loop(first, last, one_tile, 0)


def own_attention(queries, low_rank, factors, rank_width, keys, values, begin):
    tokens, width = queries.shape
    kv_local = keys.shape[1] // HEAD_WIDTH
    heads_local = width // HEAD_WIDTH
    span = PER_KV * HEAD_WIDTH
    block = min(256, tokens)
    tile = min(256, tokens)
    blocks = tokens // block
    first_tile = begin.reshape(blocks, block)[:, 0] // tile

    def body(first_ref, q_ref, lr_ref, keys_ref, v_ref, begin_ref, *refs):
        factor_refs = refs[: len(factors)]
        state_ref, adapted_ref, values_ref, acc_ref, max_ref, score_ref = refs[len(factors) :]
        step = pl.program_id(1)

        @pl.when(step == 0)
        def _():
            values_ref[:HEAD_WIDTH, :] = transposed(v_ref[...])
            values_ref[HEAD_WIDTH:, :] = jnp.ones((ONES_ROWS, tokens), jnp.bfloat16)

        up = jnp.concatenate([f[rank_width:, :] for f in factor_refs], axis=0)
        update = jnp.dot(lr_ref[...], up, preferred_element_type=jnp.float32)
        adapted = q_ref[...].astype(jnp.float32) + adapter_scale * update
        adapted_ref[...] = adapted.T.astype(jnp.bfloat16)

        acc_ref[...] = jnp.zeros_like(acc_ref)
        max_ref[...] = jnp.full_like(max_ref, UNSEEN)
        start = begin_ref[...]
        own = step * block + lax.broadcasted_iota(jnp.int32, (1, block), 1)
        heads = range(PER_KV)

        def scores_at(at):
            key_rows = keys_ref[pl.ds(at, tile), :]
            position = at + lax.broadcasted_iota(jnp.int32, (tile, block), 0)
            seen = (position >= start) & (position <= own)
            return [
                jnp.where(seen, scores_of(key_rows, adapted_ref[head_rows(h), :]), UNSEEN)
                for h in heads
            ]

        last = ((step + 1) * block + tile - 1) // tile
        visit_tiles(
            first_ref[step],
            last,
            tile,
            scores_at,
            lambda at: values_ref[:, pl.ds(at, tile)],
            score_ref,
            acc_ref,
            max_ref,
            heads,
        )
        for head in heads:
            state_ref[head, :MAX_ROW, :] = acc_ref[head, :MAX_ROW, :]
            state_ref[head, MAX_ROW:, :] = jnp.broadcast_to(
                max_ref[head : head + 1, :], (STATE_ROWS - MAX_ROW, block)
            )

    by_head = lambda h, i, first: (0, h)
    whole = pl.BlockSpec((tokens, HEAD_WIDTH), by_head)
    return pl.pallas_call(
        body,
        grid_spec=pltpu.PrefetchScalarGridSpec(
            num_scalar_prefetch=1,
            grid=(kv_local, blocks),
            in_specs=[
                pl.BlockSpec((block, span), lambda h, i, first: (i, h)),
                pl.BlockSpec((block, low_rank.shape[1]), lambda h, i, first: (i, 0)),
                whole,
                whole,
                pl.BlockSpec((1, block), lambda h, i, first: (0, i)),
            ]
            + [pl.BlockSpec((f.shape[0], span), by_head) for f in factors],
            out_specs=[
                pl.BlockSpec((PER_KV, STATE_ROWS, block), lambda h, i, first: (h, 0, i)),
                pl.BlockSpec((span, block), lambda h, i, first: (h, i)),
            ],
            scratch_shapes=[
                pltpu.VMEM((STATE_ROWS, tokens), jnp.bfloat16),
                pltpu.VMEM((PER_KV, STATE_ROWS, block), jnp.float32),
                pltpu.VMEM((8, block), jnp.float32),
                pltpu.VMEM((PER_KV, tile, block), jnp.float32),
            ],
        ),
        out_shape=[
            jax.ShapeDtypeStruct((heads_local, STATE_ROWS, tokens), jnp.float32),
            jax.ShapeDtypeStruct((width, tokens), jnp.bfloat16),
        ],
        compiler_params=pltpu.CompilerParams(vmem_limit_bytes=VMEM_LIMIT),
        cost_estimate=pl.CostEstimate(
            flops=32 * tokens * tokens * width,
            bytes_accessed=16 * 1024 * 1024,
            transcendentals=heads_local * tokens * tokens // 2,
        ),
        name="own_attention",
    )(first_tile, queries, low_rank, keys, values, begin.reshape(1, tokens), *factors)


def rest_attention(
    state, adapted, keys_before, values_before, source, begin, buffers, page_buffer
):
    width, tokens = adapted.shape
    heads_local = width // HEAD_WIDTH
    kv_local = heads_local // PER_KV
    kv_step = min(2, kv_local)
    heads_step = kv_step * PER_KV
    span = heads_step * HEAD_WIDTH
    key_span = kv_step * HEAD_WIDTH
    block = min(256, tokens)
    blocks = tokens // block
    tile = min(256, tokens)
    tiles = tokens // tile
    count = len(buffers)
    uses = jnp.any(
        page_buffer.reshape(blocks, block, 1) == jnp.arange(count)[None, None, :], axis=1
    ).astype(jnp.int32)
    first_tile = jnp.minimum(begin.reshape(blocks, block)[:, 0] // tile, tiles)
    scalars = jnp.concatenate([first_tile, source[None]])

    def body(uses_ref, first_ref, state_ref, q_ref, which_ref, begin_ref, *refs):
        keys_ref, v_refs, page_refs = refs[0], refs[1:3], refs[3 : 3 + count]
        out_ref, values_ref, before_ref, acc_ref, max_ref, score_ref = refs[3 + count :]
        step = pl.program_id(1)

        @pl.when(step == 0)
        def _():
            for b in range(count):
                for kv in range(kv_step):
                    values_ref[b, kv, :HEAD_WIDTH, :] = transposed(
                        page_refs[b][PAGE:, head_rows(kv)]
                    )
                    values_ref[b, kv, HEAD_WIDTH:, :] = jnp.ones(
                        (ONES_ROWS, PAGE), jnp.bfloat16
                    )
            for n, v_ref in enumerate(v_refs):

                @pl.when((first_ref[blocks] == n) & (first_ref[0] < tiles))
                def _():
                    for kv in range(kv_step):
                        before_ref[kv, :HEAD_WIDTH, :] = transposed(v_ref[:, head_rows(kv)])
                        before_ref[kv, HEAD_WIDTH:, :] = jnp.ones(
                            (ONES_ROWS, tokens), jnp.bfloat16
                        )

        for head in range(heads_step):
            acc_ref[head] = state_ref[head]
            max_ref[head : head + 1, :] = state_ref[head, MAX_ROW : MAX_ROW + 1, :]

        start = begin_ref[...]
        @pl.when(first_ref[step] < tiles)
        def _():
            for kv in range(kv_step):
                heads = range(kv * PER_KV, (kv + 1) * PER_KV)

                def scores_at(at):
                    key_rows = keys_ref[pl.ds(at, tile), head_rows(kv)]
                    position = at + lax.broadcasted_iota(jnp.int32, (tile, block), 0)
                    seen = position >= start
                    return [
                        jnp.where(seen, scores_of(key_rows, q_ref[head_rows(h), :]), UNSEEN)
                        for h in heads
                    ]

                visit_tiles(
                    first_ref[step],
                    tiles,
                    tile,
                    scores_at,
                    lambda at: before_ref[kv, :, pl.ds(at, tile)],
                    score_ref,
                    acc_ref,
                    max_ref,
                    heads,
                )

        which = which_ref[...]
        for b in range(count):

            @pl.when(uses_ref[step, b] != 0)
            def _():
                seen = which == b
                for kv in range(kv_step):
                    heads = range(kv * PER_KV, (kv + 1) * PER_KV)
                    key_rows = page_refs[b][:PAGE, head_rows(kv)]
                    scores = [
                        jnp.where(seen, scores_of(key_rows, q_ref[head_rows(h), :]), UNSEEN)
                        for h in heads
                    ]
                    absorb(scores, values_ref[b, kv], acc_ref, max_ref, heads)

        for head in range(heads_step):
            share = 1.0 / acc_ref[head, SUM_ROW : SUM_ROW + 1, :]
            result = acc_ref[head, :HEAD_WIDTH, :] * share
            out_ref[:, head_rows(head)] = result.T.astype(jnp.bfloat16)

    by_head = lambda h, i, uses, first: (0, h)
    by_token = pl.BlockSpec((1, block), lambda h, i, uses, first: (0, i))
    return pl.pallas_call(
        body,
        grid_spec=pltpu.PrefetchScalarGridSpec(
            num_scalar_prefetch=2,
            grid=(kv_local // kv_step, blocks),
            in_specs=[
                pl.BlockSpec(
                    (heads_step, STATE_ROWS, block), lambda h, i, uses, first: (h, 0, i)
                ),
                pl.BlockSpec((span, block), lambda h, i, uses, first: (h, i)),
                by_token,
                by_token,
            ]
            + [pl.BlockSpec((tokens, key_span), by_head)] * 3
            + [pl.BlockSpec((2 * PAGE, key_span), by_head)] * count,
            out_specs=pl.BlockSpec((block, span), lambda h, i, uses, first: (i, h)),
            scratch_shapes=[
                pltpu.VMEM((count, kv_step, STATE_ROWS, PAGE), jnp.bfloat16),
                pltpu.VMEM((kv_step, STATE_ROWS, tokens), jnp.bfloat16),
                pltpu.VMEM((heads_step, STATE_ROWS, block), jnp.float32),
                pltpu.VMEM((heads_step, block), jnp.float32),
                pltpu.VMEM((PER_KV, tile, block), jnp.float32),
            ],
        ),
        out_shape=jax.ShapeDtypeStruct((tokens, width), jnp.bfloat16),
        compiler_params=pltpu.CompilerParams(vmem_limit_bytes=VMEM_LIMIT),
        cost_estimate=pl.CostEstimate(flops=1, bytes_accessed=1, transcendentals=0),
        name="rest_attention",
    )(
        uses,
        scalars,
        state,
        adapted,
        page_buffer.reshape(1, tokens),
        begin.reshape(1, tokens),
        keys_before,
        *values_before,
        *buffers,
    )


def local(
    normed_token_input,
    queries,
    fresh_token_keys,
    fresh_token_values,
    token_request_index,
    prefix_page_cache,
    adapter_down_weight,
    adapter_up_weight,
    group_page_list,
    group_adapter_list,
    page_entry_index,
    adapter_entry_index,
):
    groups = lax.axis_size("grp")
    columns = columns_of(groups)
    rank_width = adapter_down_weight.shape[1]
    stored_pages, _, page_tokens, key_width = prefix_page_cache.shape

    onward = [(i, i + 1) for i in range(groups - 1)]
    around = [(i, i - i % columns + (i + 1) % columns) for i in range(groups)]
    first_up = [(i, i + columns) for i in range(0, groups - columns, columns)]
    starts_row = (lax.axis_index("grp") % columns == 0).astype(jnp.int32)

    adapters = jnp.concatenate([adapter_down_weight, adapter_up_weight], axis=1)
    cache = prefix_page_cache.reshape(stored_pages, 2 * page_tokens, key_width)
    adapters = Column(adapters, groups, columns)
    cache = Column(cache, groups, columns)
    adapters_next = adapters.first_step()
    values_around = lax.ppermute(fresh_token_values, "grp", around)
    cache_next = cache.first_step(adapters_next)
    (ids,) = held_until((token_request_index,), adapters_next)
    ids_before = lax.ppermute(ids + 1, "grp", onward)
    adapters.second_step()
    adapters.third_step()
    cache_after = cache.second_step()
    cache.third_step()
    factors, adapter_buffer_of = deliver(
        adapters, group_adapter_list, "adapters", (ids_before, values_around, *cache_next)
    )
    keys, values = held_until((fresh_token_keys, values_around), factors)
    keys_before = lax.ppermute(keys, "grp", onward)
    values_up = lax.ppermute(values, "grp", first_up)
    partial = low_rank_part(normed_token_input, factors, rank_width)
    if lax.axis_size("tp") == 2:
        total = partial + lax.ppermute(partial, "tp", [(0, 1), (1, 0)])
    else:
        total = lax.psum(partial, "tp")

    requests = jnp.arange(page_entry_index.shape[0], dtype=jnp.int32)
    member = token_request_index[:, None] == requests[None, :]

    def by_token(entry_index, buffer_of):
        entries = jnp.arange(buffer_of.shape[0], dtype=jnp.int32)
        chosen = jnp.sum(
            jnp.where(entry_index[:, None] == entries[None, :], buffer_of[None, :], 0), axis=1
        )
        return jnp.sum(jnp.where(member, chosen[None, :], 0), axis=1)

    def below(earlier):
        less = earlier[None, :] < token_request_index[:, None]
        return jnp.sum(less.astype(jnp.int32), axis=1)

    adapter_buffer = by_token(adapter_entry_index, adapter_buffer_of)
    lane_buffer = jnp.arange(total.shape[1], dtype=jnp.int32) // rank_width
    low_rank = jnp.where(
        adapter_buffer[:, None] == lane_buffer[None, :], total, 0.0
    ).astype(jnp.bfloat16)
    (low_rank,) = held_until((low_rank,), cache_after)
    state, adapted = own_attention(
        queries,
        low_rank,
        factors,
        rank_width,
        fresh_token_keys,
        fresh_token_values,
        below(token_request_index),
    )

    pages, page_buffer_of = deliver(
        cache, group_page_list, "pages", (adapted, keys_before, values_up)
    )
    return rest_attention(
        state,
        adapted,
        keys_before,
        (values_around, values_up),
        starts_row,
        below(ids_before - 1),
        pages,
        by_token(page_entry_index, page_buffer_of),
    )


def solution(mesh):
    placed = (
        P("grp", "tp"),
        P("grp", "tp"),
        P("grp", "tp"),
        P("grp", "tp"),
        P("grp"),
        P("grp", None, None, "tp"),
        P("grp", None, "tp"),
        P("grp", None, "tp"),
        P(),
        P(),
        P(),
        P(),
    )
    return jax.shard_map(
        local, mesh=mesh, in_specs=placed, out_specs=P("grp", "tp"), check_vma=False
    )
```

```python
import math

import jax
import jax.numpy as jnp
from jax import lax
from jax.experimental import pallas as pl
from jax.experimental.pallas import tpu as pltpu
from jax.sharding import PartitionSpec as P

QUERY_HEADS = 32
KV_HEADS = 8
HEAD_WIDTH = 128
PAGE = 128
PER_KV = QUERY_HEADS // KV_HEADS

adapter_scale = 0.5

SCORE_SCALE = HEAD_WIDTH ** (-0.5) * math.log2(math.e)
UNSEEN = -1e30

ONES_ROWS = 16
STATE_ROWS = HEAD_WIDTH + ONES_ROWS
SUM_ROW = HEAD_WIDTH
MAX_ROW = HEAD_WIDTH + 8

VMEM_LIMIT = 48 * 1024 * 1024


def columns_of(groups):
    columns = 1
    while columns * columns < groups and groups % (2 * columns) == 0:
        columns *= 2
    return columns


def held_until(arrays, others):
    together = lax.optimization_barrier(tuple(arrays) + tuple(others))
    return together[: len(arrays)]


def along_columns(steps, columns):
    return [(a * columns + c, b * columns + c) for a, b in steps for c in range(columns)]


OUTER = [(0, 1), (1, 0), (2, 3), (3, 2)]
MIDDLE = [(1, 2), (2, 1)]
ENDS = [(0, 3), (3, 0)]


class Column:

    def __init__(self, own, groups, columns):
        self.own, self.groups, self.columns = own, groups, columns
        self.rows = groups // columns

    def swap(self, shard, steps):
        return lax.ppermute(shard, "grp", along_columns(steps, self.columns))

    def first_step(self, others=()):
        if self.rows == 4:
            (own,) = held_until((self.own,), others)
            self.one, self.two = self.swap(own, OUTER), self.swap(own, MIDDLE)
            return (self.one, self.two)
        return ()

    def second_step(self):
        if self.rows == 4:
            self.three, self.four = self.swap(self.two, OUTER), self.swap(self.one, MIDDLE)
            return (self.three, self.four)
        return ()

    def end_to_end(self, others=()):
        if self.rows == 4:
            (own,) = held_until((self.own,), others)
            five = self.swap(own, ENDS)
            self.stacks = [self.own, self.one, self.two, self.three, self.four, five]
            self.table = ((0, 1, 3, 5), (1, 0, 2, 4), (4, 2, 0, 1), (5, 3, 1, 0))
            return (five,)
        rows, columns, groups = self.rows, self.columns, self.groups
        down = [(i, i + columns) for i in range(groups - columns)]
        up = [(i + columns, i) for i in range(groups - columns)]
        from_below, from_above = [], []
        lower = upper = self.own
        for _ in range(rows - 1):
            lower = lax.ppermute(lower, "grp", down)
            upper = lax.ppermute(upper, "grp", up)
            from_below.append(lower)
            from_above.append(upper)
        self.stacks = from_below[::-1] + [self.own] + from_above
        self.table = tuple(tuple(w - r + rows - 1 for w in range(rows)) for r in range(rows))
        return ()


def plan(listed, turn, stored, columns, table, name):
    groups, entries = listed.shape
    rows = groups // columns

    def body(listed_ref, turn_ref, wanted_ref, lands_ref, buffer_ref, turns_ref):
        me = lax.axis_index("grp")
        row, column = lax.div(me, columns), lax.rem(me, columns)
        turn = turn_ref[0]
        one, zero = jnp.int32(1), jnp.int32(0)

        def unit(group, entry):
            number = listed_ref[group, entry]
            owner = lax.div(number, stored)
            return lax.div(owner, columns), lax.rem(owner, columns), lax.rem(number, stored)

        def rank_of(group):
            owner_columns = [unit(group, e)[1] for e in range(entries)]
            return [
                sum(
                    [jnp.where(owner_columns[f] == owner_columns[e], one, zero) for f in range(e)],
                    zero,
                )
                for e in range(entries)
            ]

        for m in range(columns):
            partner = row * columns + jnp.bitwise_xor(column, m)
            ranks = rank_of(partner)
            stack, place = zero, zero
            for e in range(entries):
                owner_row, owner_column, within = unit(partner, e)
                here = (owner_column == column) & (ranks[e] == turn)
                held = zero
                for r in range(rows):
                    for w in range(rows):
                        held = jnp.where((row == r) & (owner_row == w), table[r][w], held)
                stack = jnp.where(here, held, stack)
                place = jnp.where(here, within, place)
            wanted_ref[m, 0] = stack
            wanted_ref[m, 1] = place

        ranks = rank_of(me)
        masks = [jnp.bitwise_xor(unit(me, e)[1], column) for e in range(entries)]
        taken = [
            sum(
                [jnp.where((ranks[e] == 0) & (masks[e] == m), one, zero) for e in range(entries)],
                zero,
            )
            for m in range(columns)
        ]
        buffers = []
        later = zero
        for e in range(entries):
            free, spare = zero, zero
            for m in range(columns):
                spare = jnp.where((taken[m] == 0) & (free == later), m, spare)
                free = free + 1 - taken[m]
            buffers.append(jnp.where(ranks[e] == 0, masks[e], spare))
            later = later + jnp.where(ranks[e] == 0, zero, one)
            buffer_ref[e] = buffers[e]
        for b in range(columns):
            lands = jnp.int32(-1)
            for e in range(entries):
                lands = jnp.where((ranks[e] == turn) & (buffers[e] == b), masks[e], lands)
            lands_ref[b] = lands

        def deepest(group, most):
            for rank in rank_of(group):
                most = jnp.maximum(most, rank + 1)
            return most

        turns_ref[0] = lax.fori_loop(0, groups, deepest, one)

    smem = pl.BlockSpec(memory_space=pltpu.SMEM)
    return pl.pallas_call(
        body,
        out_shape=[
            jax.ShapeDtypeStruct((columns, 2), jnp.int32),
            jax.ShapeDtypeStruct((columns,), jnp.int32),
            jax.ShapeDtypeStruct((entries,), jnp.int32),
            jax.ShapeDtypeStruct((1,), jnp.int32),
        ],
        in_specs=[smem, smem],
        out_specs=[smem] * 4,
        name=name,
    )(listed, turn)


def pick_units(wanted, stacks, name):
    count = wanted.shape[0]
    unit = stacks[0].shape[1:]

    def body(wanted_ref, *refs):
        sources = refs[: len(stacks)]
        outputs = refs[len(stacks) : len(stacks) + count]
        sems = refs[-1]
        for m in range(count):
            for k, source in enumerate(sources):

                @pl.when(wanted_ref[m, 0] == k)
                def _():
                    pltpu.make_async_copy(
                        source.at[wanted_ref[m, 1]], outputs[m], sems.at[m]
                    ).start()

        for m in range(count):
            pltpu.make_async_copy(sources[0].at[0], outputs[m], sems.at[m]).wait()

    return pl.pallas_call(
        body,
        out_shape=[jax.ShapeDtypeStruct(unit, stacks[0].dtype)] * count,
        in_specs=[pl.BlockSpec(memory_space=pltpu.SMEM)]
        + [pl.BlockSpec(memory_space=pl.ANY)] * len(stacks),
        out_specs=[pl.BlockSpec(memory_space=pltpu.VMEM)] * count,
        scratch_shapes=[pltpu.SemaphoreType.DMA((count,))],
        compiler_params=pltpu.CompilerParams(vmem_limit_bytes=VMEM_LIMIT),
        name=name,
    )(wanted, *stacks)


def deliver(column, listed, name, others):
    groups, columns, table = column.groups, column.columns, column.table
    stored = column.own.shape[0]
    stacks = held_until(column.stacks, others)

    def exchange(turn):
        wanted, lands, buffer_of, turns = plan(
            listed, turn, stored, columns, table, "plan_" + name
        )
        units = pick_units(wanted, stacks, "pick_" + name)
        units = [units[0]] + [
            lax.ppermute(units[m], "grp", [(i, i ^ m) for i in range(groups)])
            for m in range(1, columns)
        ]
        return units, lands, buffer_of, turns

    buffers, _, buffer_of, turns = exchange(jnp.zeros((1,), jnp.int32))

    def another(carry):
        turn, held = carry
        held = list(held)
        units, lands, _, _ = exchange(turn)
        for b in range(columns):
            for m in range(columns):
                held[b] = jnp.where(lands[b] == m, units[m], held[b])
        return turn + 1, tuple(held)

    _, buffers = lax.while_loop(
        lambda carry: carry[0][0] < turns[0],
        another,
        (jnp.ones((1,), jnp.int32), tuple(buffers)),
    )
    return buffers, buffer_of


def low_rank_part(normed, factors, rank_width):
    tokens, width = normed.shape
    block = min(256, tokens)
    total = rank_width * len(factors)

    def body(x_ref, *refs):
        down = jnp.concatenate([f[:rank_width, :] for f in refs[:-1]], axis=0)
        refs[-1][...] = lax.dot_general(
            x_ref[...], down, (((1,), (1,)), ((), ())), preferred_element_type=jnp.float32
        )

    return pl.pallas_call(
        body,
        grid=(tokens // block,),
        out_shape=jax.ShapeDtypeStruct((tokens, total), jnp.float32),
        in_specs=[pl.BlockSpec((block, width), lambda i: (i, 0))]
        + [pl.BlockSpec(f.shape, lambda i: (0, 0)) for f in factors],
        out_specs=pl.BlockSpec((block, total), lambda i: (i, 0)),
        compiler_params=pltpu.CompilerParams(vmem_limit_bytes=VMEM_LIMIT),
        cost_estimate=pl.CostEstimate(flops=1, bytes_accessed=1, transcendentals=0),
        name="low_rank_part",
    )(normed, *factors)


def scores_of(keys, queries_t):
    return jnp.dot(keys, queries_t, preferred_element_type=jnp.float32) * SCORE_SCALE


def absorb(scores, values_t, held, sums, acc_ref, max_ref):
    highest = [jnp.max(s, axis=0, keepdims=True) for s in scores]
    if held is not None:
        highest = [jnp.maximum(old, top) for old, top in zip(held, highest)]
    weights = [jnp.exp2(s - top).astype(jnp.bfloat16) for s, top in zip(scores, highest)]
    totals = [
        jnp.dot(v, w, preferred_element_type=jnp.float32) for v, w in zip(values_t, weights)
    ]
    if held is not None:
        totals = [
            total * jnp.exp2(old - top) + more
            for total, old, top, more in zip(sums, held, highest, totals)
        ]
    for n, (top, total) in enumerate(zip(highest, totals)):
        acc_ref[n] = total
        max_ref[n : n + 1, :] = top


def so_far(acc_ref, max_ref, count):
    return [max_ref[n : n + 1, :] for n in range(count)], [acc_ref[n] for n in range(count)]


def transposed(values):
    return values.T


def head_rows(head):
    return slice(head * HEAD_WIDTH, (head + 1) * HEAD_WIDTH)


def visit_tiles(first, last, tile, scores_at, values_at, score_ref, acc_ref, max_ref, fresh):
    heads = score_ref.shape[0]

    def start(number):
        return pl.multiple_of(number * tile, tile)

    def ahead_of(number):
        return scores_at(start(jnp.minimum(number + 1, last - 1)))

    def one_tile(number, scores, held, sums):
        ahead = ahead_of(number)
        absorb(scores, [values_at(start(number))] * heads, held, sums, acc_ref, max_ref)
        for n in range(heads):
            score_ref[n] = ahead[n]

    def step(number, _):
        scores = [score_ref[n] for n in range(heads)]
        one_tile(number, scores, *so_far(acc_ref, max_ref, heads))
        return 0

    scores = scores_at(start(first))
    if fresh:
        one_tile(first, scores, None, None)
        lax.fori_loop(first + 1, last, step, 0)
    else:
        for n in range(heads):
            score_ref[n] = scores[n]
        lax.fori_loop(first, last, step, 0)


def own_attention(queries, low_rank, factors, rank_width, keys, values, begin):
    tokens, width = queries.shape
    kv_local = keys.shape[1] // HEAD_WIDTH
    heads_local = width // HEAD_WIDTH
    span = PER_KV * HEAD_WIDTH
    block = min(256, tokens)
    tile = min(256, tokens)
    blocks = tokens // block
    first_tile = begin.reshape(blocks, block)[:, 0] // tile

    def body(first_ref, q_ref, lr_ref, keys_ref, v_ref, begin_ref, *refs):
        factor_refs = refs[: len(factors)]
        state_ref, adapted_ref, values_ref, max_ref, score_ref = refs[len(factors) :]
        step = pl.program_id(1)

        @pl.when(step == 0)
        def _():
            values_ref[:HEAD_WIDTH, :] = transposed(v_ref[...])
            values_ref[HEAD_WIDTH:, :] = jnp.ones((ONES_ROWS, tokens), jnp.bfloat16)

        up = jnp.concatenate([f[rank_width:, :] for f in factor_refs], axis=0)
        update = jnp.dot(lr_ref[...], up, preferred_element_type=jnp.float32)
        adapted = q_ref[...].astype(jnp.float32) + adapter_scale * update
        adapted_ref[...] = adapted.astype(jnp.bfloat16).T

        start = begin_ref[...]
        own = step * block + lax.broadcasted_iota(jnp.int32, (1, block), 1)
        heads = range(PER_KV)

        def scores_at(at):
            key_rows = keys_ref[pl.ds(at, tile), :]
            position = at + lax.broadcasted_iota(jnp.int32, (tile, block), 0)
            seen = (position >= start) & (position <= own)
            return [
                jnp.where(seen, scores_of(key_rows, adapted_ref[head_rows(h), :]), UNSEEN)
                for h in heads
            ]

        last = ((step + 1) * block + tile - 1) // tile
        visit_tiles(
            first_ref[step],
            last,
            tile,
            scores_at,
            lambda at: values_ref[:, pl.ds(at, tile)],
            score_ref,
            state_ref,
            max_ref,
            True,
        )
        for head in heads:
            state_ref[head, MAX_ROW:, :] = jnp.broadcast_to(
                max_ref[head : head + 1, :], (STATE_ROWS - MAX_ROW, block)
            )

    by_head = lambda h, i, first: (0, h)
    whole = pl.BlockSpec((tokens, HEAD_WIDTH), by_head)
    return pl.pallas_call(
        body,
        grid_spec=pltpu.PrefetchScalarGridSpec(
            num_scalar_prefetch=1,
            grid=(kv_local, blocks),
            in_specs=[
                pl.BlockSpec((block, span), lambda h, i, first: (i, h)),
                pl.BlockSpec((block, low_rank.shape[1]), lambda h, i, first: (i, 0)),
                whole,
                whole,
                pl.BlockSpec((1, block), lambda h, i, first: (0, i)),
            ]
            + [pl.BlockSpec((f.shape[0], span), by_head) for f in factors],
            out_specs=[
                pl.BlockSpec((PER_KV, STATE_ROWS, block), lambda h, i, first: (h, 0, i)),
                pl.BlockSpec((span, block), lambda h, i, first: (h, i)),
            ],
            scratch_shapes=[
                pltpu.VMEM((STATE_ROWS, tokens), jnp.bfloat16),
                pltpu.VMEM((8, block), jnp.float32),
                pltpu.VMEM((PER_KV, tile, block), jnp.float32),
            ],
        ),
        out_shape=[
            jax.ShapeDtypeStruct((heads_local, STATE_ROWS, tokens), jnp.float32),
            jax.ShapeDtypeStruct((width, tokens), jnp.bfloat16),
        ],
        compiler_params=pltpu.CompilerParams(vmem_limit_bytes=VMEM_LIMIT),
        cost_estimate=pl.CostEstimate(
            flops=32 * tokens * tokens * width,
            bytes_accessed=16 * 1024 * 1024,
            transcendentals=0,
        ),
        name="own_attention",
    )(first_tile, queries, low_rank, keys, values, begin.reshape(1, tokens), *factors)


def rest_attention(
    state, adapted, keys_before, values_before, source, begin, buffers, page_buffer
):
    width, tokens = adapted.shape
    heads_local = width // HEAD_WIDTH
    kv_local = heads_local // PER_KV
    kv_step = min(2, kv_local)
    heads_step = kv_step * PER_KV
    span = heads_step * HEAD_WIDTH
    key_span = kv_step * HEAD_WIDTH
    block = min(256, tokens)
    blocks = tokens // block
    tile = min(256, tokens)
    tiles = tokens // tile
    count = len(buffers)
    numbers = jnp.arange(count, dtype=jnp.int32)
    needs = jnp.any(page_buffer.reshape(blocks, block, 1) == numbers, axis=1)
    place = jnp.sum(
        (needs[:, None, :] & (numbers[None, :] < numbers[:, None])[None]).astype(jnp.int32), axis=2
    )
    lists = jnp.sum(
        jnp.where(needs[:, None, :] & (place[:, None, :] == numbers[:, None]), numbers, 0), axis=2
    )
    uses = jnp.concatenate(
        [lists, jnp.sum(needs.astype(jnp.int32), axis=1, keepdims=True)], axis=1
    )
    first_tile = jnp.minimum(begin.reshape(blocks, block)[:, 0] // tile, tiles)
    scalars = jnp.concatenate([first_tile, source[None]])

    def body(uses_ref, first_ref, state_ref, q_ref, which_ref, begin_ref, *refs):
        keys_ref, v_refs, page_refs = refs[0], refs[1:3], refs[3 : 3 + count]
        out_ref, page_keys_ref, values_ref, before_ref, acc_ref, max_ref, score_ref = refs[
            3 + count :
        ]
        step = pl.program_id(1)

        @pl.when(step == 0)
        def _():
            for b in range(count):
                for kv in range(kv_step):
                    page_keys_ref[b, kv] = page_refs[b][:PAGE, head_rows(kv)]
                    values_ref[b, kv, :HEAD_WIDTH, :] = transposed(
                        page_refs[b][PAGE:, head_rows(kv)]
                    )
                    values_ref[b, kv, HEAD_WIDTH:, :] = jnp.ones(
                        (ONES_ROWS, PAGE), jnp.bfloat16
                    )
            for n, v_ref in enumerate(v_refs):

                @pl.when((first_ref[blocks] == n) & (first_ref[0] < tiles))
                def _():
                    for kv in range(kv_step):
                        before_ref[kv, :HEAD_WIDTH, :] = transposed(v_ref[:, head_rows(kv)])
                        before_ref[kv, HEAD_WIDTH:, :] = jnp.ones(
                            (ONES_ROWS, tokens), jnp.bfloat16
                        )

        which = which_ref[...]

        def one_page(number, held, sums):
            b = uses_ref[step, number]
            seen = which == b
            scores = [
                jnp.where(
                    seen,
                    scores_of(page_keys_ref[b, h // PER_KV], q_ref[head_rows(h), :]),
                    UNSEEN,
                )
                for h in range(heads_step)
            ]
            values_t = [values_ref[b, h // PER_KV] for h in range(heads_step)]
            absorb(scores, values_t, held, sums, acc_ref, max_ref)

        held = [state_ref[h, MAX_ROW : MAX_ROW + 1, :] for h in range(heads_step)]
        one_page(0, held, [state_ref[h] for h in range(heads_step)])

        def another_page(number, _):
            one_page(number, *so_far(acc_ref, max_ref, heads_step))
            return 0

        lax.fori_loop(1, uses_ref[step, count], another_page, 0)

        start = begin_ref[...]
        @pl.when(first_ref[step] < tiles)
        def _():
            for kv in range(kv_step):
                heads = range(kv * PER_KV, (kv + 1) * PER_KV)

                def scores_at(at):
                    key_rows = keys_ref[pl.ds(at, tile), head_rows(kv)]
                    position = at + lax.broadcasted_iota(jnp.int32, (tile, block), 0)
                    seen = position >= start
                    return [
                        jnp.where(seen, scores_of(key_rows, q_ref[head_rows(h), :]), UNSEEN)
                        for h in heads
                    ]

                visit_tiles(
                    first_ref[step],
                    tiles,
                    tile,
                    scores_at,
                    lambda at: before_ref[kv, :, pl.ds(at, tile)],
                    score_ref,
                    acc_ref.at[pl.ds(kv * PER_KV, PER_KV)],
                    max_ref.at[pl.ds(kv * PER_KV, PER_KV)],
                    False,
                )

        for head in range(heads_step):
            share = 1.0 / acc_ref[head, SUM_ROW : SUM_ROW + 1, :]
            result = acc_ref[head, :HEAD_WIDTH, :] * share
            out_ref[:, head_rows(head)] = result.astype(jnp.bfloat16).T

    by_head = lambda h, i, uses, first: (0, h)
    by_token = pl.BlockSpec((1, block), lambda h, i, uses, first: (0, i))
    return pl.pallas_call(
        body,
        grid_spec=pltpu.PrefetchScalarGridSpec(
            num_scalar_prefetch=2,
            grid=(kv_local // kv_step, blocks),
            in_specs=[
                pl.BlockSpec(
                    (heads_step, STATE_ROWS, block), lambda h, i, uses, first: (h, 0, i)
                ),
                pl.BlockSpec((span, block), lambda h, i, uses, first: (h, i)),
                by_token,
                by_token,
            ]
            + [pl.BlockSpec((tokens, key_span), by_head)] * 3
            + [pl.BlockSpec((2 * PAGE, key_span), by_head)] * count,
            out_specs=pl.BlockSpec((block, span), lambda h, i, uses, first: (i, h)),
            scratch_shapes=[
                pltpu.VMEM((count, kv_step, PAGE, HEAD_WIDTH), jnp.bfloat16),
                pltpu.VMEM((count, kv_step, STATE_ROWS, PAGE), jnp.bfloat16),
                pltpu.VMEM((kv_step, STATE_ROWS, tokens), jnp.bfloat16),
                pltpu.VMEM((heads_step, STATE_ROWS, block), jnp.float32),
                pltpu.VMEM((heads_step, block), jnp.float32),
                pltpu.VMEM((PER_KV, tile, block), jnp.float32),
            ],
        ),
        out_shape=jax.ShapeDtypeStruct((tokens, width), jnp.bfloat16),
        compiler_params=pltpu.CompilerParams(vmem_limit_bytes=VMEM_LIMIT),
        cost_estimate=pl.CostEstimate(flops=1, bytes_accessed=1, transcendentals=0),
        name="rest_attention",
    )(
        uses,
        scalars,
        state,
        adapted,
        page_buffer.reshape(1, tokens),
        begin.reshape(1, tokens),
        keys_before,
        *values_before,
        *buffers,
    )


def local(
    normed_token_input,
    queries,
    fresh_token_keys,
    fresh_token_values,
    token_request_index,
    prefix_page_cache,
    adapter_down_weight,
    adapter_up_weight,
    group_page_list,
    group_adapter_list,
    page_entry_index,
    adapter_entry_index,
):
    groups = lax.axis_size("grp")
    columns = columns_of(groups)
    rank_width = adapter_down_weight.shape[1]
    stored_pages, _, page_tokens, key_width = prefix_page_cache.shape

    onward = [(i, i + 1) for i in range(groups - 1)]
    around = [(i, i - i % columns + (i + 1) % columns) for i in range(groups)]
    first_up = [(i, i + columns) for i in range(0, groups - columns, columns)]
    starts_row = (lax.axis_index("grp") % columns == 0).astype(jnp.int32)

    adapters = jnp.concatenate([adapter_down_weight, adapter_up_weight], axis=1)
    cache = prefix_page_cache.reshape(stored_pages, 2 * page_tokens, key_width)
    adapters = Column(adapters, groups, columns)
    cache = Column(cache, groups, columns)
    adapters_next = adapters.first_step()
    values_around = lax.ppermute(fresh_token_values, "grp", around)
    cache_next = cache.first_step(adapters_next)
    (ids,) = held_until((token_request_index,), adapters_next)
    ids_before = lax.ppermute(ids + 1, "grp", onward)
    adapters.second_step()
    adapters.end_to_end()
    cache_after = cache.second_step()
    cache.end_to_end(cache_next)
    factors, adapter_buffer_of = deliver(
        adapters, group_adapter_list, "adapters", (ids_before, values_around, *cache_next)
    )
    keys, values = held_until((fresh_token_keys, values_around), factors)
    keys_before = lax.ppermute(keys, "grp", onward)
    values_up = lax.ppermute(values, "grp", first_up)
    (normed,) = held_until((normed_token_input,), cache_after)
    partial = low_rank_part(normed, factors, rank_width)
    if lax.axis_size("tp") == 2:
        total = partial + lax.ppermute(partial, "tp", [(0, 1), (1, 0)])
    else:
        total = lax.psum(partial, "tp")

    requests = jnp.arange(page_entry_index.shape[0], dtype=jnp.int32)
    member = token_request_index[:, None] == requests[None, :]

    def by_token(entry_index, buffer_of):
        entries = jnp.arange(buffer_of.shape[0], dtype=jnp.int32)
        chosen = jnp.sum(
            jnp.where(entry_index[:, None] == entries[None, :], buffer_of[None, :], 0), axis=1
        )
        return jnp.sum(jnp.where(member, chosen[None, :], 0), axis=1)

    def below(earlier):
        less = earlier[None, :] < token_request_index[:, None]
        return jnp.sum(less.astype(jnp.int32), axis=1)

    adapter_buffer = by_token(adapter_entry_index, adapter_buffer_of)
    lane_buffer = jnp.arange(total.shape[1], dtype=jnp.int32) // rank_width
    low_rank = jnp.where(
        adapter_buffer[:, None] == lane_buffer[None, :], total, 0.0
    ).astype(jnp.bfloat16)
    state, adapted = own_attention(
        queries,
        low_rank,
        factors,
        rank_width,
        fresh_token_keys,
        fresh_token_values,
        below(token_request_index),
    )

    pages, page_buffer_of = deliver(
        cache, group_page_list, "pages", (adapted, keys_before, values_up)
    )
    return rest_attention(
        state,
        adapted,
        keys_before,
        (values_around, values_up),
        starts_row,
        below(ids_before - 1),
        pages,
        by_token(page_entry_index, page_buffer_of),
    )


def solution(mesh):
    placed = (
        P("grp", "tp"),
        P("grp", "tp"),
        P("grp", "tp"),
        P("grp", "tp"),
        P("grp"),
        P("grp", None, None, "tp"),
        P("grp", None, "tp"),
        P("grp", None, "tp"),
        P(),
        P(),
        P(),
        P(),
    )
    return jax.shard_map(
        local, mesh=mesh, in_specs=placed, out_specs=P("grp", "tp"), check_vma=False
    )
```

```python
import math

import jax
import jax.numpy as jnp
from jax import lax
from jax.experimental import pallas as pl
from jax.experimental.pallas import tpu as pltpu
from jax.sharding import PartitionSpec as P

QUERY_HEADS = 32
KV_HEADS = 8
HEAD_WIDTH = 128
PAGE = 128
PER_KV = QUERY_HEADS // KV_HEADS

adapter_scale = 0.5

SCORE_SCALE = HEAD_WIDTH ** (-0.5) * math.log2(math.e)
UNSEEN = -1e30

ONES_ROWS = 16
STATE_ROWS = HEAD_WIDTH + ONES_ROWS
SUM_ROW = HEAD_WIDTH
MAX_ROW = HEAD_WIDTH + 8

VMEM_LIMIT = 48 * 1024 * 1024


def columns_of(groups):
    columns = 1
    while columns * columns < groups and groups % (2 * columns) == 0:
        columns *= 2
    return columns


def held_until(arrays, others):
    together = lax.optimization_barrier(tuple(arrays) + tuple(others))
    return together[: len(arrays)]


def along_columns(steps, columns):
    return [(a * columns + c, b * columns + c) for a, b in steps for c in range(columns)]


OUTER = [(0, 1), (1, 0), (2, 3), (3, 2)]
MIDDLE = [(1, 2), (2, 1)]
ENDS = [(0, 3), (3, 0)]


class Column:

    def __init__(self, own, groups, columns):
        self.own, self.groups, self.columns = own, groups, columns
        self.rows = groups // columns

    def swap(self, shard, steps):
        return lax.ppermute(shard, "grp", along_columns(steps, self.columns))

    def first_step(self, others=()):
        if self.rows == 4:
            (own,) = held_until((self.own,), others)
            self.one, self.two = self.swap(own, OUTER), self.swap(own, MIDDLE)
            return (self.one, self.two)
        return ()

    def second_step(self):
        if self.rows == 4:
            self.three, self.four = self.swap(self.two, OUTER), self.swap(self.one, MIDDLE)
            return (self.three, self.four)
        return ()

    def end_to_end(self, others=()):
        if self.rows == 4:
            (own,) = held_until((self.own,), others)
            five = self.swap(own, ENDS)
            self.stacks = [self.own, self.one, self.two, self.three, self.four, five]
            self.table = ((0, 1, 3, 5), (1, 0, 2, 4), (4, 2, 0, 1), (5, 3, 1, 0))
            return (five,)
        rows, columns, groups = self.rows, self.columns, self.groups
        down = [(i, i + columns) for i in range(groups - columns)]
        up = [(i + columns, i) for i in range(groups - columns)]
        from_below, from_above = [], []
        lower = upper = self.own
        for _ in range(rows - 1):
            lower = lax.ppermute(lower, "grp", down)
            upper = lax.ppermute(upper, "grp", up)
            from_below.append(lower)
            from_above.append(upper)
        self.stacks = from_below[::-1] + [self.own] + from_above
        self.table = tuple(tuple(w - r + rows - 1 for w in range(rows)) for r in range(rows))
        return ()


def plan(listed, turn, stored, columns, table, name):
    groups, entries = listed.shape
    rows = groups // columns

    def body(listed_ref, turn_ref, wanted_ref, lands_ref, buffer_ref, turns_ref):
        me = lax.axis_index("grp")
        row, column = lax.div(me, columns), lax.rem(me, columns)
        turn = turn_ref[0]
        one, zero = jnp.int32(1), jnp.int32(0)

        def unit(group, entry):
            number = listed_ref[group, entry]
            owner = lax.div(number, stored)
            return lax.div(owner, columns), lax.rem(owner, columns), lax.rem(number, stored)

        def rank_of(group):
            owner_columns = [unit(group, e)[1] for e in range(entries)]
            return [
                sum(
                    [jnp.where(owner_columns[f] == owner_columns[e], one, zero) for f in range(e)],
                    zero,
                )
                for e in range(entries)
            ]

        for m in range(columns):
            partner = row * columns + m
            ranks = rank_of(partner)
            stack, place = zero, zero
            for e in range(entries):
                owner_row, owner_column, within = unit(partner, e)
                here = (owner_column == column) & (ranks[e] == turn)
                held = zero
                for r in range(rows):
                    for w in range(rows):
                        held = jnp.where((row == r) & (owner_row == w), table[r][w], held)
                stack = jnp.where(here, held, stack)
                place = jnp.where(here, within, place)
            wanted_ref[m, 0] = stack
            wanted_ref[m, 1] = place

        ranks = rank_of(me)
        sources = [unit(me, e)[1] for e in range(entries)]
        taken = [
            sum(
                [jnp.where((ranks[e] == 0) & (sources[e] == m), one, zero) for e in range(entries)],
                zero,
            )
            for m in range(columns)
        ]
        buffers = []
        later = zero
        for e in range(entries):
            free, spare = zero, zero
            for m in range(columns):
                spare = jnp.where((taken[m] == 0) & (free == later), m, spare)
                free = free + 1 - taken[m]
            buffers.append(jnp.where(ranks[e] == 0, sources[e], spare))
            later = later + jnp.where(ranks[e] == 0, zero, one)
            buffer_ref[e] = buffers[e]
        for b in range(columns):
            lands = jnp.int32(-1)
            for e in range(entries):
                lands = jnp.where((ranks[e] == turn) & (buffers[e] == b), sources[e], lands)
            lands_ref[b] = lands

        def deepest(group, most):
            for rank in rank_of(group):
                most = jnp.maximum(most, rank + 1)
            return most

        turns_ref[0] = lax.fori_loop(0, groups, deepest, one)

    smem = pl.BlockSpec(memory_space=pltpu.SMEM)
    return pl.pallas_call(
        body,
        out_shape=[
            jax.ShapeDtypeStruct((columns, 2), jnp.int32),
            jax.ShapeDtypeStruct((columns,), jnp.int32),
            jax.ShapeDtypeStruct((entries,), jnp.int32),
            jax.ShapeDtypeStruct((1,), jnp.int32),
        ],
        in_specs=[smem, smem],
        out_specs=[smem] * 4,
        name=name,
    )(listed, turn)


def pick_units(wanted, stacks, name):
    count = wanted.shape[0]
    unit = stacks[0].shape[1:]

    def body(wanted_ref, *refs):
        sources = refs[: len(stacks)]
        output, sems = refs[len(stacks) :]
        for m in range(count):
            for k, source in enumerate(sources):

                @pl.when(wanted_ref[m, 0] == k)
                def _():
                    pltpu.make_async_copy(
                        source.at[wanted_ref[m, 1]], output.at[m], sems.at[m]
                    ).start()

        for m in range(count):
            pltpu.make_async_copy(sources[0].at[0], output.at[m], sems.at[m]).wait()

    return pl.pallas_call(
        body,
        out_shape=jax.ShapeDtypeStruct((count,) + unit, stacks[0].dtype),
        in_specs=[pl.BlockSpec(memory_space=pltpu.SMEM)]
        + [pl.BlockSpec(memory_space=pl.ANY)] * len(stacks),
        out_specs=pl.BlockSpec(memory_space=pltpu.VMEM),
        scratch_shapes=[pltpu.SemaphoreType.DMA((count,))],
        compiler_params=pltpu.CompilerParams(vmem_limit_bytes=VMEM_LIMIT),
        name=name,
    )(wanted, *stacks)


def deliver(column, listed, name, others):
    groups, columns, table = column.groups, column.columns, column.table
    stored = column.own.shape[0]
    stacks = held_until(column.stacks, others)

    rows_of = [list(range(r, r + columns)) for r in range(0, groups, columns)]

    def exchange(turn):
        wanted, lands, buffer_of, turns = plan(
            listed, turn, stored, columns, table, "plan_" + name
        )
        units = pick_units(wanted, stacks, "pick_" + name)
        units = lax.all_to_all(units, "grp", 0, 0, axis_index_groups=rows_of, tiled=True)
        return units, lands, buffer_of, turns

    buffers, _, buffer_of, turns = exchange(jnp.zeros((1,), jnp.int32))

    def another(carry):
        turn, held = carry
        units, lands, _, _ = exchange(turn)
        for b in range(columns):
            for m in range(columns):
                held = held.at[b].set(jnp.where(lands[b] == m, units[m], held[b]))
        return turn + 1, held

    def finish(buffers):
        _, buffers = lax.while_loop(
            lambda carry: carry[0][0] < turns[0],
            another,
            (jnp.ones((1,), jnp.int32), buffers),
        )
        return buffers

    return buffers, buffer_of, finish


def low_rank_part(normed, factors, rank_width):
    tokens, width = normed.shape
    block = min(256, tokens)
    count = factors.shape[0]
    total = rank_width * count

    def body(x_ref, f_ref, out_ref):
        down = jnp.concatenate([f_ref[n, :rank_width, :] for n in range(count)], axis=0)
        out_ref[...] = lax.dot_general(
            x_ref[...], down, (((1,), (1,)), ((), ())), preferred_element_type=jnp.float32
        )

    return pl.pallas_call(
        body,
        grid=(tokens // block,),
        out_shape=jax.ShapeDtypeStruct((tokens, total), jnp.float32),
        in_specs=[
            pl.BlockSpec((block, width), lambda i: (i, 0)),
            pl.BlockSpec(factors.shape, lambda i: (0, 0, 0)),
        ],
        out_specs=pl.BlockSpec((block, total), lambda i: (i, 0)),
        compiler_params=pltpu.CompilerParams(vmem_limit_bytes=VMEM_LIMIT),
        cost_estimate=pl.CostEstimate(flops=1, bytes_accessed=1, transcendentals=0),
        name="low_rank_part",
    )(normed, factors)


def scores_of(keys, queries_t):
    return jnp.dot(keys, queries_t, preferred_element_type=jnp.float32) * SCORE_SCALE


def absorb(scores, values_t, held, sums, acc_ref, max_ref):
    highest = [jnp.max(s, axis=0, keepdims=True) for s in scores]
    if held is not None:
        highest = [jnp.maximum(old, top) for old, top in zip(held, highest)]
    weights = [jnp.exp2(s - top).astype(jnp.bfloat16) for s, top in zip(scores, highest)]
    totals = [
        jnp.dot(v, w, preferred_element_type=jnp.float32) for v, w in zip(values_t, weights)
    ]
    if held is not None:
        totals = [
            total * jnp.exp2(old - top) + more
            for total, old, top, more in zip(sums, held, highest, totals)
        ]
    for n, (top, total) in enumerate(zip(highest, totals)):
        acc_ref[n] = total
        max_ref[n : n + 1, :] = top


def so_far(acc_ref, max_ref, count):
    return [max_ref[n : n + 1, :] for n in range(count)], [acc_ref[n] for n in range(count)]


def transposed(values):
    return values.T


def head_rows(head):
    return slice(head * HEAD_WIDTH, (head + 1) * HEAD_WIDTH)


def visit_tiles(first, last, tile, scores_at, values_at, score_ref, acc_ref, max_ref, fresh):
    heads = score_ref.shape[0]

    def start(number):
        return pl.multiple_of(number * tile, tile)

    def ahead_of(number):
        return scores_at(start(jnp.minimum(number + 1, last - 1)))

    def one_tile(number, scores, held, sums):
        ahead = ahead_of(number)
        absorb(scores, [values_at(start(number))] * heads, held, sums, acc_ref, max_ref)
        for n in range(heads):
            score_ref[n] = ahead[n]

    def step(number, _):
        scores = [score_ref[n] for n in range(heads)]
        one_tile(number, scores, *so_far(acc_ref, max_ref, heads))
        return 0

    scores = scores_at(start(first))
    if fresh:
        one_tile(first, scores, None, None)
        lax.fori_loop(first + 1, last, step, 0)
    else:
        for n in range(heads):
            score_ref[n] = scores[n]
        lax.fori_loop(first, last, step, 0)


def own_attention(queries, low_rank, factors, rank_width, keys, values, begin):
    tokens, width = queries.shape
    kv_local = keys.shape[1] // HEAD_WIDTH
    heads_local = width // HEAD_WIDTH
    span = PER_KV * HEAD_WIDTH
    block = min(256, tokens)
    tile = min(256, tokens)
    blocks = tokens // block
    count = factors.shape[0]
    first_tile = begin.reshape(blocks, block)[:, 0] // tile

    def body(first_ref, q_ref, lr_ref, keys_ref, v_ref, begin_ref, f_ref, *refs):
        state_ref, adapted_ref, values_ref, max_ref, score_ref = refs
        step = pl.program_id(1)

        @pl.when(step == 0)
        def _():
            values_ref[:HEAD_WIDTH, :] = transposed(v_ref[...])
            values_ref[HEAD_WIDTH:, :] = jnp.ones((ONES_ROWS, tokens), jnp.bfloat16)

        up = jnp.concatenate([f_ref[n, rank_width:, :] for n in range(count)], axis=0)
        update = jnp.dot(lr_ref[...], up, preferred_element_type=jnp.float32)
        adapted = q_ref[...].astype(jnp.float32) + adapter_scale * update
        adapted_ref[...] = adapted.astype(jnp.bfloat16).T

        start = begin_ref[...]
        own = step * block + lax.broadcasted_iota(jnp.int32, (1, block), 1)
        heads = range(PER_KV)

        def scores_at(at):
            key_rows = keys_ref[pl.ds(at, tile), :]
            position = at + lax.broadcasted_iota(jnp.int32, (tile, block), 0)
            seen = (position >= start) & (position <= own)
            return [
                jnp.where(seen, scores_of(key_rows, adapted_ref[head_rows(h), :]), UNSEEN)
                for h in heads
            ]

        last = ((step + 1) * block + tile - 1) // tile
        visit_tiles(
            first_ref[step],
            last,
            tile,
            scores_at,
            lambda at: values_ref[:, pl.ds(at, tile)],
            score_ref,
            state_ref,
            max_ref,
            True,
        )
        for head in heads:
            state_ref[head, MAX_ROW:, :] = jnp.broadcast_to(
                max_ref[head : head + 1, :], (STATE_ROWS - MAX_ROW, block)
            )

    by_head = lambda h, i, first: (0, h)
    whole = pl.BlockSpec((tokens, HEAD_WIDTH), by_head)
    return pl.pallas_call(
        body,
        grid_spec=pltpu.PrefetchScalarGridSpec(
            num_scalar_prefetch=1,
            grid=(kv_local, blocks),
            in_specs=[
                pl.BlockSpec((block, span), lambda h, i, first: (i, h)),
                pl.BlockSpec((block, low_rank.shape[1]), lambda h, i, first: (i, 0)),
                whole,
                whole,
                pl.BlockSpec((1, block), lambda h, i, first: (0, i)),
                pl.BlockSpec((count, factors.shape[1], span), lambda h, i, first: (0, 0, h)),
            ],
            out_specs=[
                pl.BlockSpec((PER_KV, STATE_ROWS, block), lambda h, i, first: (h, 0, i)),
                pl.BlockSpec((span, block), lambda h, i, first: (h, i)),
            ],
            scratch_shapes=[
                pltpu.VMEM((STATE_ROWS, tokens), jnp.bfloat16),
                pltpu.VMEM((8, block), jnp.float32),
                pltpu.VMEM((PER_KV, tile, block), jnp.float32),
            ],
        ),
        out_shape=[
            jax.ShapeDtypeStruct((heads_local, STATE_ROWS, tokens), jnp.float32),
            jax.ShapeDtypeStruct((width, tokens), jnp.bfloat16),
        ],
        compiler_params=pltpu.CompilerParams(vmem_limit_bytes=VMEM_LIMIT),
        cost_estimate=pl.CostEstimate(
            flops=32 * tokens * tokens * width,
            bytes_accessed=16 * 1024 * 1024,
            transcendentals=0,
        ),
        name="own_attention",
    )(first_tile, queries, low_rank, keys, values, begin.reshape(1, tokens), factors)


def rest_attention(
    state, adapted, keys_before, values_before, source, begin, buffers, page_buffer
):
    width, tokens = adapted.shape
    heads_local = width // HEAD_WIDTH
    kv_local = heads_local // PER_KV
    kv_step = min(2, kv_local)
    heads_step = kv_step * PER_KV
    span = heads_step * HEAD_WIDTH
    key_span = kv_step * HEAD_WIDTH
    block = min(256, tokens)
    blocks = tokens // block
    tile = min(256, tokens)
    tiles = tokens // tile
    count = buffers.shape[0]
    numbers = jnp.arange(count, dtype=jnp.int32)
    needs = jnp.any(page_buffer.reshape(blocks, block, 1) == numbers, axis=1)
    place = jnp.sum(
        (needs[:, None, :] & (numbers[None, :] < numbers[:, None])[None]).astype(jnp.int32), axis=2
    )
    lists = jnp.sum(
        jnp.where(needs[:, None, :] & (place[:, None, :] == numbers[:, None]), numbers, 0), axis=2
    )
    uses = jnp.concatenate(
        [lists, jnp.sum(needs.astype(jnp.int32), axis=1, keepdims=True)], axis=1
    )
    first_tile = jnp.minimum(begin.reshape(blocks, block)[:, 0] // tile, tiles)
    scalars = jnp.concatenate([first_tile, source[None]])

    def body(uses_ref, first_ref, state_ref, q_ref, which_ref, begin_ref, *refs):
        keys_ref, v_refs, page_ref = refs[0], refs[1:3], refs[3]
        out_ref, page_keys_ref, values_ref, before_ref, acc_ref, max_ref, score_ref = refs[4:]
        step = pl.program_id(1)

        @pl.when(step == 0)
        def _():
            for b in range(count):
                for kv in range(kv_step):
                    page_keys_ref[b, kv] = page_ref[b, :PAGE, head_rows(kv)]
                    values_ref[b, kv, :HEAD_WIDTH, :] = transposed(
                        page_ref[b, PAGE:, head_rows(kv)]
                    )
                    values_ref[b, kv, HEAD_WIDTH:, :] = jnp.ones(
                        (ONES_ROWS, PAGE), jnp.bfloat16
                    )
            for n, v_ref in enumerate(v_refs):

                @pl.when((first_ref[blocks] == n) & (first_ref[0] < tiles))
                def _():
                    for kv in range(kv_step):
                        before_ref[kv, :HEAD_WIDTH, :] = transposed(v_ref[:, head_rows(kv)])
                        before_ref[kv, HEAD_WIDTH:, :] = jnp.ones(
                            (ONES_ROWS, tokens), jnp.bfloat16
                        )

        which = which_ref[...]

        def one_page(number, held, sums):
            b = uses_ref[step, number]
            seen = which == b
            scores = [
                jnp.where(
                    seen,
                    scores_of(page_keys_ref[b, h // PER_KV], q_ref[head_rows(h), :]),
                    UNSEEN,
                )
                for h in range(heads_step)
            ]
            values_t = [values_ref[b, h // PER_KV] for h in range(heads_step)]
            absorb(scores, values_t, held, sums, acc_ref, max_ref)

        held = [state_ref[h, MAX_ROW : MAX_ROW + 1, :] for h in range(heads_step)]
        one_page(0, held, [state_ref[h] for h in range(heads_step)])

        def another_page(number, _):
            one_page(number, *so_far(acc_ref, max_ref, heads_step))
            return 0

        lax.fori_loop(1, uses_ref[step, count], another_page, 0)

        start = begin_ref[...]
        @pl.when(first_ref[step] < tiles)
        def _():
            for kv in range(kv_step):
                heads = range(kv * PER_KV, (kv + 1) * PER_KV)

                def scores_at(at):
                    key_rows = keys_ref[pl.ds(at, tile), head_rows(kv)]
                    position = at + lax.broadcasted_iota(jnp.int32, (tile, block), 0)
                    seen = position >= start
                    return [
                        jnp.where(seen, scores_of(key_rows, q_ref[head_rows(h), :]), UNSEEN)
                        for h in heads
                    ]

                visit_tiles(
                    first_ref[step],
                    tiles,
                    tile,
                    scores_at,
                    lambda at: before_ref[kv, :, pl.ds(at, tile)],
                    score_ref,
                    acc_ref.at[pl.ds(kv * PER_KV, PER_KV)],
                    max_ref.at[pl.ds(kv * PER_KV, PER_KV)],
                    False,
                )

        for head in range(heads_step):
            share = 1.0 / acc_ref[head, SUM_ROW : SUM_ROW + 1, :]
            result = acc_ref[head, :HEAD_WIDTH, :] * share
            out_ref[:, head_rows(head)] = result.astype(jnp.bfloat16).T

    by_head = lambda h, i, uses, first: (0, h)
    by_token = pl.BlockSpec((1, block), lambda h, i, uses, first: (0, i))
    return pl.pallas_call(
        body,
        grid_spec=pltpu.PrefetchScalarGridSpec(
            num_scalar_prefetch=2,
            grid=(kv_local // kv_step, blocks),
            in_specs=[
                pl.BlockSpec(
                    (heads_step, STATE_ROWS, block), lambda h, i, uses, first: (h, 0, i)
                ),
                pl.BlockSpec((span, block), lambda h, i, uses, first: (h, i)),
                by_token,
                by_token,
            ]
            + [pl.BlockSpec((tokens, key_span), by_head)] * 3
            + [pl.BlockSpec((count, 2 * PAGE, key_span), lambda h, i, uses, first: (0, 0, h))],
            out_specs=pl.BlockSpec((block, span), lambda h, i, uses, first: (i, h)),
            scratch_shapes=[
                pltpu.VMEM((count, kv_step, PAGE, HEAD_WIDTH), jnp.bfloat16),
                pltpu.VMEM((count, kv_step, STATE_ROWS, PAGE), jnp.bfloat16),
                pltpu.VMEM((kv_step, STATE_ROWS, tokens), jnp.bfloat16),
                pltpu.VMEM((heads_step, STATE_ROWS, block), jnp.float32),
                pltpu.VMEM((heads_step, block), jnp.float32),
                pltpu.VMEM((PER_KV, tile, block), jnp.float32),
            ],
        ),
        out_shape=jax.ShapeDtypeStruct((tokens, width), jnp.bfloat16),
        compiler_params=pltpu.CompilerParams(vmem_limit_bytes=VMEM_LIMIT),
        cost_estimate=pl.CostEstimate(flops=1, bytes_accessed=1, transcendentals=0),
        name="rest_attention",
    )(
        uses,
        scalars,
        state,
        adapted,
        page_buffer.reshape(1, tokens),
        begin.reshape(1, tokens),
        keys_before,
        *values_before,
        buffers,
    )


def local(
    normed_token_input,
    queries,
    fresh_token_keys,
    fresh_token_values,
    token_request_index,
    prefix_page_cache,
    adapter_down_weight,
    adapter_up_weight,
    group_page_list,
    group_adapter_list,
    page_entry_index,
    adapter_entry_index,
):
    groups = lax.axis_size("grp")
    columns = columns_of(groups)
    rank_width = adapter_down_weight.shape[1]
    stored_pages, _, page_tokens, key_width = prefix_page_cache.shape

    onward = [(i, i + 1) for i in range(groups - 1)]
    around = [(i, i - i % columns + (i + 1) % columns) for i in range(groups)]
    first_up = [(i, i + columns) for i in range(0, groups - columns, columns)]
    starts_row = (lax.axis_index("grp") % columns == 0).astype(jnp.int32)

    adapters = jnp.concatenate([adapter_down_weight, adapter_up_weight], axis=1)
    cache = prefix_page_cache.reshape(stored_pages, 2 * page_tokens, key_width)
    adapters = Column(adapters, groups, columns)
    cache = Column(cache, groups, columns)
    adapters_next = adapters.first_step()
    values_around = lax.ppermute(fresh_token_values, "grp", around)
    adapters_after = adapters.second_step()
    adapters.end_to_end()
    cache.first_step(adapters_after)
    cache.second_step()
    cache.end_to_end(adapters_next)
    factors, adapter_buffer_of, finish = deliver(
        adapters, group_adapter_list, "adapters", (values_around,)
    )
    factors = finish(factors)
    keys, values = held_until((fresh_token_keys, values_around), (factors,))
    keys_before = lax.ppermute(keys, "grp", onward)
    values_up = lax.ppermute(values, "grp", first_up)
    partial = low_rank_part(normed_token_input, factors, rank_width)
    if lax.axis_size("tp") == 2:
        total = partial + lax.ppermute(partial, "tp", [(0, 1), (1, 0)])
    else:
        total = lax.psum(partial, "tp")

    requests = jnp.arange(page_entry_index.shape[0], dtype=jnp.int32)
    member = token_request_index[:, None] == requests[None, :]

    def by_token(entry_index, buffer_of):
        entries = jnp.arange(buffer_of.shape[0], dtype=jnp.int32)
        chosen = jnp.sum(
            jnp.where(entry_index[:, None] == entries[None, :], buffer_of[None, :], 0), axis=1
        )
        return jnp.sum(jnp.where(member, chosen[None, :], 0), axis=1)

    def below(earlier):
        less = earlier[None, :] < token_request_index[:, None]
        return jnp.sum(less.astype(jnp.int32), axis=1)

    adapter_buffer = by_token(adapter_entry_index, adapter_buffer_of)
    lane_buffer = jnp.arange(total.shape[1], dtype=jnp.int32) // rank_width
    low_rank = jnp.where(
        adapter_buffer[:, None] == lane_buffer[None, :], total, 0.0
    ).astype(jnp.bfloat16)
    (ids,) = held_until((token_request_index,), (total,))
    ids_before = lax.ppermute(ids + 1, "grp", onward)
    pages, page_buffer_of, finish = deliver(cache, group_page_list, "pages", (total,))
    state, adapted = own_attention(
        queries,
        low_rank,
        factors,
        rank_width,
        fresh_token_keys,
        fresh_token_values,
        below(token_request_index),
    )

    (pages,) = held_until((pages,), (adapted,))
    pages = finish(pages)
    return rest_attention(
        state,
        adapted,
        keys_before,
        (values_around, values_up),
        starts_row,
        below(ids_before - 1),
        pages,
        by_token(page_entry_index, page_buffer_of),
    )


def solution(mesh):
    placed = (
        P("grp", "tp"),
        P("grp", "tp"),
        P("grp", "tp"),
        P("grp", "tp"),
        P("grp"),
        P("grp", None, None, "tp"),
        P("grp", None, "tp"),
        P("grp", None, "tp"),
        P(),
        P(),
        P(),
        P(),
    )
    return jax.shard_map(
        local, mesh=mesh, in_specs=placed, out_specs=P("grp", "tp"), check_vma=False
    )
```
